512 devices in a mesh: segment: 8 (over y, core), expert: 64 (over x, z).
Axes of the slice: x: 4, y: 4, z: 16, core: 2. Of those that a mesh axis runs over, the one named last changes fastest.
Arguments:
- hidden: bfloat16 [8, 2048, 2048], P('segment', 'expert'), may hold values from -6 to 6
- memory: bfloat16 [8, 2048, 2048], P('segment', 'expert'), may hold values from -6 to 6
- lengths: int32 [8, 64], P('segment', 'expert'), may hold values from 1 to 32, as said below
- memory_lengths: int32 [8, 64], P('segment', 'expert'), may hold values from 1 to 32, as said below
- routes: int32 [8, 2048, 2], P('segment', 'expert'), may hold values from 0 to 3, all different within a row; in each aligned block of 32 rows (0 to 31, 32 to 63, ..., all dimensions but the last counted through in order) at most 20 rows name the same one
- norm_gain: float32 [8, 3, 2048], P('segment'), may hold values from 0.5 to 1.5, as said below
- router: bfloat16 [8, 2048, 4], P('segment'), may hold values from -0.26516504 to 0.26516504, as said below
- w_in: bfloat16 [8, 2048, 16384], P('segment', None, 'expert'), may hold values from -0.13258252 to 0.13258252, as said below
- w_out: bfloat16 [8, 16384, 2048], P('segment', 'expert'), may hold values from -0.125 to 0.125, as said below
- shortlist: bfloat16 [8, 2048, 512], P('segment'), may hold values from -0.375 to 0.375
- student: float32 [8, 2048, 512], P('segment', 'expert'), may hold values from -15 to 15
- targets: int32 [8, 2048], P('segment', 'expert'), may hold values from 0 to 511
Outputs:
- layer_out: bfloat16 [8, 2048, 2048], P('segment', 'expert')
- loss: float32 [], replicated
The draws below stay inside these ranges and needn't reach their ends.
Inputs may be any that keep to these rules, and one draw needn't show every extreme that they name: `lengths`: every sequence has at least one position; the first sequence of each section has 32. `memory_lengths`: every sequence has at least one position; the first sequence of each section has 32. `routes`: A token's two experts differ. In the 32 rows of one device no expert is named more than 20 times, a bound that some block reaches. `norm_gain`: equal in all encoder sections, and equal in all decoder sections. `router`: equal in all encoder sections, and equal in all decoder sections. `w_in`: equal in all encoder sections, and equal in all decoder sections. `w_out`: equal in all encoder sections, and equal in all decoder sections.
All inputs are finite; a program needn't handle non-finite values.
Results may differ from the reference program's by a relative error of at most 0.0049.
Values may be sent and summed in bfloat16 or wider, within the bound.
No kernel may reach another device: no remote copies, remote signals or barrier semaphores. Data moves between devices by JAX's collectives and lax.ppermute only.
A program may use at most 64 MiB of HBM per device.

```python
import math
import jax
import jax.numpy as jnp
import numpy as np
from jax import lax

D = 2048
HEADS = 16
HEAD_DIM = 128
FF = 4096
EXPERTS = 4
VOCW = 512
LEN = 32
TOK_DEV = 32
CAP = 20
SEQS = 64
TOKENS = 2048
N_SEGMENT = 8
N_EXPERT = 64


def lengths_common(key):
    drawn = jax.random.randint(key, (N_SEGMENT, SEQS), 1, LEN + 1)
    return drawn.at[:, 0].set(LEN).astype(jnp.int32)


def draw_lengths(key, part):
    return lengths_common(jax.random.fold_in(key, 11))


def draw_memory_lengths(key, part):
    return lengths_common(jax.random.fold_in(key, 12))


def shared_sets(key, shape, scale, limit):
    drawn = jnp.clip(jax.random.normal(key, (2,) + shape, jnp.float32) * scale, -limit, limit)
    return jnp.repeat(drawn, N_SEGMENT // 2, axis=0)


def draw_norm_gain(key, part):
    spread = shared_sets(jax.random.fold_in(key, 21), (3, D), 0.1, 0.5)
    return (1.0 + spread).astype(jnp.float32)


def draw_router(key, part):
    return shared_sets(jax.random.fold_in(key, 22), (D, EXPERTS), 2.0 / math.sqrt(D), 12.0 / math.sqrt(D)).astype(jnp.bfloat16)


def draw_w_in(key, part):
    return shared_sets(jax.random.fold_in(key, 23), (D, EXPERTS * FF), 1.0 / math.sqrt(D), 6.0 / math.sqrt(D)).astype(jnp.bfloat16)


def draw_w_out(key, part):
    return shared_sets(jax.random.fold_in(key, 24), (EXPERTS * FF, D), math.sqrt(2.0 / FF), 8.0 / math.sqrt(FF)).astype(jnp.bfloat16)


def plant(values, rng, smallest, largest):
    longest = values.shape.index(max(values.shape))
    spots = []
    for shift in (0, 1):
        where = [jax.random.randint(jax.random.fold_in(rng, axis), (), 0, length) for axis, length in enumerate(values.shape)]
        where[longest] = (where[longest] + shift) % values.shape[longest]
        spots.append(tuple(where))
    return values.at[spots[0]].set(smallest).at[spots[1]].set(largest)


def shard_levels(rng, dims, pieces, low, top_value):
    def one(position, shards_of):
        steps = jax.random.uniform(jax.random.fold_in(jax.random.fold_in(rng, 6), position), (shards_of,), jnp.float32, low / len(pieces), top_value / len(pieces))
        return jnp.repeat(jnp.exp(steps), dims[position] // shards_of).reshape((-1,) + (1,) * (len(dims) - position - 1))

    level = one(*pieces[0])
    for cut in pieces[1:]:
        level = level * one(*cut)
    return level


def deal_out(own_key, own, number, rows, count, top, most, skew):
    order = jax.random.permutation(own_key, count)
    heavy_load, usual = portions_of(count, rows * top, most, skew, True), portions_of(count, rows * top, most, skew, False)
    places = jnp.arange(count)

    def named(sizes, offset_by):
        used = int((sizes > 0).sum())
        fixed = max(1, used // 4)
        shifted = fixed + (places - fixed + offset_by * (used - fixed)) % max(1, count - fixed)
        return jnp.zeros((count,), jnp.int32).at[order[jnp.where(places < fixed, places, shifted)]].set(jnp.asarray(sizes, jnp.int32))

    sizes = jnp.where(number % 4 == 0, named(heavy_load, number // 4), named(usual, number - number // 4 - 1))
    mixed = jax.random.permutation(jax.random.fold_in(own, 3), count)
    giver, taker = mixed[0:count // 2 * 2:2], mixed[1:count // 2 * 2:2]
    slack = jnp.minimum(sizes[giver] - 1, most - sizes[taker]) // 2
    slack = jnp.where((giver == order[0]) | (taker == order[0]) | (sizes[taker] == 0), 0, jnp.maximum(slack, 0))
    shifted = jax.random.randint(jax.random.fold_in(own, 4), (count // 2,), 0, 1 << 20) % (slack + 1)
    sizes = sizes.at[giver].add(-shifted).at[taker].add(shifted)
    items = jnp.searchsorted(jnp.cumsum(sizes), jnp.arange(rows * top), side="right").astype(jnp.int32)
    grid = items.reshape(top, rows).T
    grid = grid[jax.random.permutation(jax.random.fold_in(own, 1), rows)]
    offset_by = jax.random.randint(jax.random.fold_in(own, 2), (rows, 1), 0, top)
    return jnp.take_along_axis(grid, (jnp.arange(top)[None, :] + offset_by) % top, axis=1)


def portions_of(number_of, total, bound, lean, full):
    weights = [(1 << 20) // math.isqrt(standing ** lean) + 1 for standing in range(1, number_of + 1)]
    largest = bound if full else min(bound, max(-(-total // number_of), total * weights[0] // sum(weights)))
    least = 1 if total - largest >= number_of - 1 else 0
    given, surplus = [largest] + [least] * (number_of - 1), total - largest - least * (number_of - 1)
    while surplus > 0:
        movable = [i for i in range(1, number_of) if given[i] < largest] or [i for i in range(1, number_of) if given[i] < bound]
        pool, remaining = sum([weights[i] for i in movable]), surplus
        for i in movable:
            more = min(bound - given[i], max(1, remaining * weights[i] // pool), surplus)
            given[i] = given[i] + more
            surplus = surplus - more
    return np.array(given)


def noise(rng, shape, deviation, bound, pieces=(), held_as=jnp.bfloat16):
    loudness = shard_levels(rng, shape, pieces, -0.22, 0.18) if pieces else 1.0
    values = jax.random.normal(rng, shape, jnp.float32) * deviation * loudness
    return jnp.minimum(jnp.maximum(values, -bound), bound).astype(held_as)


def setup_inputs(seed: int = 0) -> dict:
    seeds = jax.random.split(jax.random.key(seed), 13)
    hidden = noise(seeds[0], (N_SEGMENT, TOKENS, D), 1.0, 6.0, ((0, 8), (1, 64)))
    memory = noise(seeds[1], (N_SEGMENT, TOKENS, D), 1.0, 6.0, ((0, 8), (1, 64)))
    lengths = draw_lengths(jax.random.fold_in(seeds[12], 71), 0)
    memory_lengths = draw_memory_lengths(jax.random.fold_in(seeds[12], 71), 0)
    routes_keys = jax.random.split(jax.random.fold_in(seeds[4], 1), N_SEGMENT * TOKENS // TOK_DEV)
    routes_turns = jax.random.permutation(jax.random.fold_in(seeds[4], 3), N_SEGMENT * TOKENS // TOK_DEV)
    routes = jax.vmap(lambda own, number: deal_out(jax.random.fold_in(seeds[4], 2), own, number, TOK_DEV, EXPERTS, 2, CAP, 2))(routes_keys, routes_turns).reshape((N_SEGMENT, TOKENS, 2))
    norm_gain = draw_norm_gain(jax.random.fold_in(seeds[12], 71), 0)
    router = draw_router(jax.random.fold_in(seeds[12], 71), 0)
    w_in = draw_w_in(jax.random.fold_in(seeds[12], 71), 0)
    w_out = draw_w_out(jax.random.fold_in(seeds[12], 71), 0)
    shortlist = noise(seeds[9], (N_SEGMENT, D, VOCW), (D // 9) ** -0.5, 0.375, ((0, 8),))
    student = noise(seeds[10], (N_SEGMENT, TOKENS, VOCW), 3.0, 15.0, ((0, 8), (1, 64)), jnp.float32)
    targets = plant(jax.random.randint(seeds[11], (N_SEGMENT, TOKENS), 0, VOCW), jax.random.fold_in(seeds[11], 1), 0, VOCW - 1).astype(jnp.int32)
    return {"hidden": hidden, "memory": memory, "lengths": lengths, "memory_lengths": memory_lengths, "routes": routes, "norm_gain": norm_gain, "router": router, "w_in": w_in, "w_out": w_out, "shortlist": shortlist, "student": student, "targets": targets}


epsilon = 1e-05

def layer_norm(values, gain_row):
    centred = values - lax.optimization_barrier(jnp.mean(values, axis=-1, keepdims=True))
    spread = lax.optimization_barrier(jnp.mean(centred * centred, axis=-1, keepdims=True))
    return centred * lax.rsqrt(spread + epsilon) * gain_row

def round_trip(values):
    return lax.optimization_barrier(values.astype(jnp.bfloat16)).astype(jnp.float32)

def reference(hidden, memory, lengths, memory_lengths, routes, norm_gain, router, w_in, w_out, shortlist, student, targets):
    half_segments = N_SEGMENT // 2
    group_size = N_EXPERT // EXPERTS
    part_width = FF // group_size
    tokens = hidden.shape[1]
    positions = jnp.arange(tokens) % LEN
    seq_index = jnp.arange(tokens) // LEN
    expert_ids = jnp.arange(EXPERTS)
    score_scale = 1.0 / math.sqrt(HEAD_DIM)
    outputs = []
    loss_sum = jnp.zeros((), jnp.float32)
    loss_count = jnp.zeros((), jnp.float32)
    for section in range(N_SEGMENT):
        states = hidden[section].astype(jnp.float32)
        is_valid = positions < lengths[section][seq_index]
        if section >= half_segments:
            source = section - half_segments
            key_rows = memory[source]
            allowed = positions < memory_lengths[source][seq_index]
            queries = layer_norm(states, norm_gain[section, 0]).astype(jnp.bfloat16)
            query_heads = queries.reshape(SEQS, LEN, HEADS, HEAD_DIM).astype(jnp.float32)
            key_heads = key_rows.reshape(SEQS, LEN, HEADS, HEAD_DIM).astype(jnp.float32)
            scores = jnp.einsum('bqhd,bkhd->bhqk', query_heads, key_heads) * score_scale
            scores = jnp.where(allowed.reshape(SEQS, 1, 1, LEN), scores, -1e+30)
            weights = round_trip(jax.nn.softmax(scores, axis=-1))
            attended = jnp.einsum('bhqk,bkhd->bqhd', weights, key_heads).reshape(tokens, D)
            mid_states = states + attended
        else:
            mid_states = states
        normed = layer_norm(mid_states, norm_gain[section, 1]).astype(jnp.bfloat16)
        router_probs = jax.nn.softmax(jnp.dot(normed, router[section], preferred_element_type=jnp.float32), axis=-1)
        first_hot = (routes[section][:, 0:1] == expert_ids).astype(jnp.float32)
        second = (routes[section][:, 1:2] == expert_ids).astype(jnp.float32)
        prob_first = lax.optimization_barrier(jnp.sum(router_probs * first_hot, axis=-1, keepdims=True))
        prob_second = lax.optimization_barrier(jnp.sum(router_probs * second, axis=-1, keepdims=True))
        prob_total = prob_first + prob_second
        gate_rows = (prob_first * first_hot + prob_second * second) / prob_total
        combine_rows = gate_rows * is_valid[:, None].astype(jnp.float32)
        first_stack = w_in[section].reshape(D, EXPERTS, FF).transpose(1, 0, 2)
        second_stack = w_out[section].reshape(EXPERTS, group_size, part_width, D)

        def expert_step(running, stacked):
            first_weight, second_weight, share_col = stacked
            activated = jnp.maximum(jnp.dot(normed, first_weight, preferred_element_type=jnp.float32), 0.0)
            activated = round_trip(activated).reshape(tokens, group_size, part_width)
            parts = jnp.einsum('tgf,gfd->tgd', activated, second_weight.astype(jnp.float32))
            parts = round_trip(parts)
            return (running + share_col[:, None] * lax.optimization_barrier(jnp.sum(parts, axis=1)), None)
        moe_out, _ = lax.scan(expert_step, jnp.zeros((tokens, D), jnp.float32), (first_stack, second_stack, combine_rows.T))
        layer_out = (mid_states + moe_out).astype(jnp.bfloat16)
        outputs.append(layer_out)
        if section >= half_segments:
            final_normed = layer_norm(layer_out.astype(jnp.float32), norm_gain[section, 2]).astype(jnp.bfloat16)
            teacher = jax.nn.log_softmax(jnp.dot(final_normed, shortlist[section], preferred_element_type=jnp.float32), axis=-1)
            learner = jax.nn.log_softmax(student[section], axis=-1)
            picked = (targets[section][:, None] == jnp.arange(VOCW)).astype(jnp.float32)
            token_loss = lax.optimization_barrier(jnp.sum(jnp.exp(teacher) * (teacher - learner), axis=-1)) - lax.optimization_barrier(jnp.sum(picked * learner, axis=-1))
            counted = is_valid.astype(jnp.float32)
            loss_sum = loss_sum + jnp.sum(token_loss * counted)
            loss_count = loss_count + jnp.sum(counted)
    return (jnp.stack(outputs), loss_sum / loss_count)
```

```python
import math

import jax
import jax.numpy as jnp
from jax import lax
from jax.sharding import Mesh, PartitionSpec as P

HEADS = 16
HEAD_DIM = 128
LEN = 32


epsilon = 1e-05


def passed_along(block, axis, distance):
    devices = range(lax.axis_size(axis))
    route = [(i - distance, i) for i in devices if i - distance in devices]
    return lax.ppermute(block, axis, route)


def layer_norm(values, gain_row):
    centred = values - jnp.mean(values, axis=-1, keepdims=True)
    spread = jnp.mean(centred * centred, axis=-1, keepdims=True)
    return centred * lax.rsqrt(spread + epsilon) * gain_row


def expert_rows(rows, first_weight, second_weight):
    activated = jnp.maximum(
        jnp.dot(rows, first_weight, preferred_element_type=jnp.float32), 0.0
    ).astype(jnp.bfloat16)
    return jnp.dot(activated, second_weight, preferred_element_type=jnp.float32).astype(
        jnp.bfloat16
    )


def local(
    hidden,
    memory,
    lengths,
    memory_lengths,
    routes,
    norm_gain,
    router,
    w_in,
    w_out,
    shortlist,
    student,
    targets,
):
    chips = lax.axis_size("y")
    experts = router.shape[2]
    tok_rows = hidden.shape[1]
    model_width = hidden.shape[2]
    capacity = 5 * tok_rows // 8
    decoder = lax.axis_index("y") >= chips // 2
    positions = jnp.arange(tok_rows) % LEN
    seq_index = jnp.arange(tok_rows) // LEN
    is_valid = positions < lengths[0][seq_index]
    key_mask = (positions < memory_lengths[0][seq_index]).astype(jnp.bfloat16)
    arrived, arrived_mask = passed_along((memory[0], key_mask), "y", chips // 2)
    states = hidden[0].astype(jnp.float32)
    gain_rows = norm_gain[0]
    seq_count = tok_rows // LEN
    score_scale = 1.0 / math.sqrt(HEAD_DIM)
    queries = (
        layer_norm(states, gain_rows[0])
        .astype(jnp.bfloat16)
        .reshape(seq_count, LEN, HEADS, HEAD_DIM)
    )
    key_rows = arrived.reshape(seq_count, LEN, HEADS, HEAD_DIM)
    scores = (
        jnp.einsum("bqhd,bkhd->bhqk", queries, key_rows, preferred_element_type=jnp.float32)
        * score_scale
    )
    allowed = arrived_mask.reshape(seq_count, 1, 1, LEN) > 0.5
    scores = jnp.where(allowed, scores, -1e30)
    weights = jax.nn.softmax(scores, axis=-1).astype(jnp.bfloat16)
    attended = jnp.einsum(
        "bhqk,bkhd->bqhd", weights, key_rows, preferred_element_type=jnp.float32
    ).reshape(tok_rows, model_width)
    mid_states = states + jnp.where(decoder, attended, 0.0)
    normed = layer_norm(mid_states, gain_rows[1]).astype(jnp.bfloat16)
    router_probs = jax.nn.softmax(
        jnp.dot(normed, router[0], preferred_element_type=jnp.float32), axis=-1
    )
    expert_ids = jnp.arange(experts)
    first_hot = (routes[0][:, 0:1] == expert_ids).astype(jnp.float32)
    second = (routes[0][:, 1:2] == expert_ids).astype(jnp.float32)
    prob_first = jnp.sum(router_probs * first_hot, axis=-1, keepdims=True)
    prob_second = jnp.sum(router_probs * second, axis=-1, keepdims=True)
    prob_total = prob_first + prob_second
    gate_rows = (prob_first * first_hot + prob_second * second) / prob_total
    chosen = (first_hot + second) * is_valid[:, None].astype(jnp.float32)
    upto = (jnp.arange(tok_rows)[:, None] >= jnp.arange(tok_rows)[None, :]).astype(jnp.float32)
    slot_rank = jnp.dot(upto, chosen, preferred_element_type=jnp.float32) - 1.0
    slot_ids = jnp.arange(capacity).astype(jnp.float32)
    placing = chosen.T[:, None, :] * (slot_rank.T[:, None, :] == slot_ids[None, :, None]).astype(
        jnp.float32
    )
    buffer = jnp.einsum(
        "ect,td->ecd", placing.astype(jnp.bfloat16), normed, preferred_element_type=jnp.float32
    ).astype(jnp.bfloat16)
    at_expert = lax.all_to_all(buffer, "x", split_axis=0, concat_axis=0, tiled=True)
    rows = lax.all_gather(
        at_expert.reshape(experts * capacity, model_width), "z", axis=0, tiled=True
    )
    partial_out = expert_rows(rows, w_in[0], w_out[0])
    expert_sum = lax.psum_scatter(partial_out, "z", scatter_dimension=0, tiled=True)
    summed = lax.all_to_all(
        expert_sum.reshape(experts, capacity, model_width), "x", split_axis=0, concat_axis=0, tiled=True
    ).astype(jnp.float32)
    weighting = placing * gate_rows.T[:, None, :]
    moe_out = jnp.einsum("ect,ecd->td", weighting, summed, precision=lax.Precision.HIGHEST)
    layer_out = (mid_states + moe_out).astype(jnp.bfloat16)
    final_normed = layer_norm(layer_out.astype(jnp.float32), gain_rows[2]).astype(jnp.bfloat16)
    teacher = jax.nn.log_softmax(
        jnp.dot(final_normed, shortlist[0], preferred_element_type=jnp.float32), axis=-1
    )
    learner = jax.nn.log_softmax(student[0], axis=-1)
    picked = (targets[0][:, None] == jnp.arange(student.shape[2])).astype(jnp.float32)
    token_loss = jnp.sum(jnp.exp(teacher) * (teacher - learner), axis=-1) - jnp.sum(
        picked * learner, axis=-1
    )
    counted = jnp.where(decoder, is_valid.astype(jnp.float32), 0.0)
    totals = jnp.stack([jnp.sum(token_loss * counted), jnp.sum(counted)])
    for axis in ("z", "x", "y", "core"):
        totals = lax.psum(totals, axis)
    return (layer_out[None], totals[0] / totals[1])


def solution(mesh):
    segments, expert_devices = mesh.devices.shape
    experts = 4
    fine = Mesh(
        mesh.devices.reshape(segments // 2, 2, experts, expert_devices // experts),
        ("y", "core", "x", "z"),
    )
    seg, exp = ("y", "core"), ("x", "z")
    placed = (
        P(seg, exp, None),
        P(seg, exp, None),
        P(seg, exp),
        P(seg, exp),
        P(seg, exp, None),
        P(seg, None, None),
        P(seg, None, None),
        P(seg, None, exp),
        P(seg, exp, None),
        P(seg, None, None),
        P(seg, exp, None),
        P(seg, exp),
    )
    return jax.shard_map(
        local,
        mesh=fine,
        in_specs=placed,
        out_specs=(P(seg, exp, None), P()),
        check_vma=False,
    )
```

```python
import functools
import math

import jax
import jax.numpy as jnp
from jax import lax
from jax.experimental import pallas as pl
from jax.experimental.pallas import tpu as pltpu
from jax.sharding import Mesh, PartitionSpec as P

HEADS = 16
HEAD_DIM = 128
LEN = 32
ZL = 4


epsilon = 1e-05
f32, bf16 = jnp.float32, jnp.bfloat16


def passed_along(block, axis, distance):
    devices = range(lax.axis_size(axis))
    route = [(i - distance, i) for i in devices if i - distance in devices]
    return lax.ppermute(block, axis, route)


def turned(block, axis, distance):
    count = math.prod(lax.axis_size(a) for a in ([axis] if isinstance(axis, str) else axis))
    return lax.ppermute(block, axis, [(i, (i + distance) % count) for i in range(count)])


def layer_norm(values, gain_row):
    centred = values - jnp.mean(values, axis=-1, keepdims=True)
    spread = jnp.mean(centred * centred, axis=-1, keepdims=True)
    return centred * lax.rsqrt(spread + epsilon) * gain_row


def kernel_call(body, out_shape, in_specs, cost, limit=40 << 20):
    whole = pl.BlockSpec(memory_space=pltpu.VMEM)
    scalar = pl.BlockSpec(memory_space=pltpu.SMEM)
    return pl.pallas_call(
        body,
        out_shape=out_shape,
        in_specs=[scalar if k == "s" else whole for k in in_specs],
        out_specs=jax.tree.map(lambda _: whole, out_shape),
        cost_estimate=pl.CostEstimate(flops=cost[0], bytes_accessed=cost[1], transcendentals=0),
        compiler_params=pltpu.CompilerParams(vmem_limit_bytes=limit),
    )


def share_body(core, w_in, w_out, out):
    width, hidden = w_in.shape
    half, deep = hidden // 2, width // 2

    @pl.when(core[0] == 0)
    def _():
        for h in range(2):
            for d in range(2):
                out[h, :, d * half : (d + 1) * half] = w_in[
                    d * deep : (d + 1) * deep, h * half : (h + 1) * half
                ]

    @pl.when(core[0] != 0)
    def _():
        for h in range(2):
            for p in range(width // hidden):
                out[h, p * half : (p + 1) * half, :] = w_out[
                    h * half : (h + 1) * half, p * hidden : (p + 1) * hidden
                ]


def mlp_body(core, rows, w_in, w_out, up0, dn0, fu0, fd0, up1, dn1, fu1, fd1, out, acc):
    width, hidden = w_in.shape
    half, deep = hidden // 2, width // 2

    def hidden_of(product):
        return jnp.maximum(product, 0.0).astype(bf16)

    first = hidden_of(jnp.dot(rows[...], w_in[...], preferred_element_type=f32))
    acc[...] = jnp.dot(first, w_out[...], preferred_element_type=f32)

    def pair(in_a, in_b, out_a, out_b):
        low = jnp.concatenate([in_a[:, :half], in_b[:, :half]], axis=1)
        high = jnp.concatenate([in_a[:, half:], in_b[:, half:]], axis=1)
        act = hidden_of(
            jnp.dot(rows[:, :deep], low, preferred_element_type=f32)
            + jnp.dot(rows[:, deep:], high, preferred_element_type=f32)
        )
        for p in range(width // hidden):
            at = slice(p * half, (p + 1) * half)
            panel = jnp.concatenate([out_a[at, :], out_b[at, :]], axis=0)
            cols = slice(p * hidden, (p + 1) * hidden)
            acc[:, cols] += jnp.dot(act, panel, preferred_element_type=f32)

    def rest(a, b):
        for k in range(2):
            pair(a[k].at[0], a[k].at[1], b[k].at[0], b[k].at[1])
        pair(a[2], a[3], b[2], b[3])

    mine, other = (up0, dn0, fu0, fd0), (up1, dn1, fu1, fd1)

    @pl.when(core[0] == 0)
    def _():
        rest(mine, other)

    @pl.when(core[0] != 0)
    def _():
        rest(other, mine)

    out[...] = acc[...].astype(bf16)


def pack_body(slots, own, b1, b2, b3, rows, high, low):
    width = rows.shape[1]
    lanes = rows.shape[0]
    tokens = jnp.concatenate([own[...], b1[...], b2[...], b3[...]], axis=0)
    count = tokens.shape[0]
    aux = tokens[:, width:]
    lane = lax.broadcasted_iota(jnp.int32, (128, lanes), 1)
    part = lax.broadcasted_iota(jnp.int32, (128, lanes), 0)
    of_expert = lane // slots
    pick_high = (part == of_expert).astype(f32).astype(bf16)
    pick_low = (part == of_expert + 8).astype(f32).astype(bf16)
    gate_high = jnp.dot(aux, pick_high, preferred_element_type=f32)
    gate_low = jnp.dot(aux, pick_low, preferred_element_type=f32)
    chosen = gate_high > 0.0
    upto = (
        lax.broadcasted_iota(jnp.int32, (count, count), 0)
        >= lax.broadcasted_iota(jnp.int32, (count, count), 1)
    ).astype(f32).astype(bf16)
    rank = jnp.dot(upto, chosen.astype(f32).astype(bf16), preferred_element_type=f32)
    slot = (lax.broadcasted_iota(jnp.int32, (count, lanes), 1) % slots + 1).astype(f32)
    here = jnp.where(chosen & (rank == slot), 1.0, 0.0)
    rows[...] = lax.dot_general(
        here.astype(bf16), tokens[:, :width], (((0,), (0,)), ((), ())), preferred_element_type=f32
    ).astype(bf16)
    high[...] = (here * gate_high).astype(bf16)
    low[...] = (here * gate_low).astype(bf16)


def combine_body(rows, high, low, own, o1, o2, o3):
    value = jnp.dot(high[...], rows[...], preferred_element_type=f32) + jnp.dot(
        low[...], rows[...], preferred_element_type=f32
    )
    n = own.shape[0]
    own[...] = value[:n]
    for k, o in enumerate((o1, o2, o3)):
        o[...] = value[(k + 1) * n : (k + 2) * n].astype(bf16)


def local(
    hidden,
    memory,
    lengths,
    memory_lengths,
    routes,
    norm_gain,
    router,
    w_in,
    w_out,
    shortlist,
    student,
    targets,
):
    chips = lax.axis_size("y")
    experts = router.shape[2]
    tok_rows = hidden.shape[1]
    model_width = hidden.shape[2]
    capacity = 5 * tok_rows // 8
    decoder = lax.axis_index("y") >= chips // 2
    positions = jnp.arange(tok_rows) % LEN
    seq_index = jnp.arange(tok_rows) // LEN
    is_valid = positions < lengths[0][seq_index]
    key_mask = (positions < memory_lengths[0][seq_index]).astype(jnp.bfloat16)
    arrived, arrived_mask = passed_along((memory[0], key_mask), "y", chips // 2)
    core = lax.axis_index("core").astype(jnp.int32)[None]
    model_hidden = w_in.shape[2]
    shared = kernel_call(
        share_body,
        jax.ShapeDtypeStruct((2, model_width // 2, model_hidden), bf16),
        "svv",
        (0, 3 << 20),
    )(core, w_in[0], w_out[0])
    line = ("z4", "zl")
    up, down = turned(shared, line, -1), turned(shared, line, 1)
    far_up, far_down = turned(up[0], line, -1), turned(down[1], line, 1)
    mine = (up, down, far_up, far_down)
    other = [turned(piece, "core", 1) for piece in mine]
    states = hidden[0].astype(jnp.float32)
    gain_rows = norm_gain[0]
    seq_count = tok_rows // LEN
    score_scale = 1.0 / math.sqrt(HEAD_DIM)
    queries = (
        layer_norm(states, gain_rows[0])
        .astype(jnp.bfloat16)
        .reshape(seq_count, LEN, HEADS, HEAD_DIM)
    )
    key_rows = arrived.reshape(seq_count, LEN, HEADS, HEAD_DIM)
    scores = (
        jnp.einsum("bqhd,bkhd->bhqk", queries, key_rows, preferred_element_type=jnp.float32)
        * score_scale
    )
    allowed = arrived_mask.reshape(seq_count, 1, 1, LEN) > 0.5
    scores = jnp.where(allowed, scores, -1e30)
    weights = jax.nn.softmax(scores, axis=-1).astype(jnp.bfloat16)
    attended = jnp.einsum(
        "bhqk,bkhd->bqhd", weights, key_rows, preferred_element_type=jnp.float32
    ).reshape(tok_rows, model_width)
    mid_states = states + jnp.where(decoder, attended, 0.0)
    normed = layer_norm(mid_states, gain_rows[1]).astype(jnp.bfloat16)
    router_probs = jax.nn.softmax(
        jnp.dot(normed, router[0], preferred_element_type=jnp.float32), axis=-1
    )
    expert_ids = jnp.arange(experts)
    first_hot = (routes[0][:, 0:1] == expert_ids).astype(jnp.float32)
    second = (routes[0][:, 1:2] == expert_ids).astype(jnp.float32)
    prob_first = jnp.sum(router_probs * first_hot, axis=-1, keepdims=True)
    prob_second = jnp.sum(router_probs * second, axis=-1, keepdims=True)
    prob_total = prob_first + prob_second
    gate_rows = (prob_first * first_hot + prob_second * second) / prob_total
    combine = gate_rows * (first_hot + second) * is_valid[:, None].astype(f32)
    combine_high = combine.astype(bf16)
    combine_low = (combine - lax.reduce_precision(combine, 8, 7)).astype(bf16)
    pad = jnp.zeros((tok_rows, 8 - experts), bf16)
    block = jnp.concatenate(
        [normed, combine_high, pad, combine_low, pad, jnp.zeros((tok_rows, 112), bf16)], axis=1
    )
    visitors = [turned(block, "z4", k) for k in (1, 2, 3)]
    slots = 4 * capacity
    lanes = experts * slots
    packed, gates_high, gates_low = kernel_call(
        functools.partial(pack_body, slots),
        (
            jax.ShapeDtypeStruct((lanes, model_width), bf16),
            jax.ShapeDtypeStruct((4 * tok_rows, lanes), bf16),
            jax.ShapeDtypeStruct((4 * tok_rows, lanes), bf16),
        ),
        "vvvv",
        (2 * lanes * 4 * tok_rows * model_width, 2 << 20),
    )(block, *visitors)
    rows = lax.all_to_all(packed, "x", split_axis=0, concat_axis=0, tiled=True)
    whole = pl.BlockSpec(memory_space=pltpu.VMEM)
    partial_out = pl.pallas_call(
        mlp_body,
        out_shape=jax.ShapeDtypeStruct((lanes, model_width), bf16),
        in_specs=[pl.BlockSpec(memory_space=pltpu.SMEM)] + [whole] * 11,
        out_specs=whole,
        scratch_shapes=[pltpu.VMEM((lanes, model_width), f32)],
        cost_estimate=pl.CostEstimate(
            flops=4 * lanes * model_width * 1024, bytes_accessed=11 << 20, transcendentals=0
        ),
        compiler_params=pltpu.CompilerParams(vmem_limit_bytes=40 << 20),
    )(core, rows, w_in[0], w_out[0], *mine, *other)
    returned = lax.all_to_all(partial_out, "x", split_axis=0, concat_axis=0, tiled=True)
    own_part, *parts = kernel_call(
        combine_body,
        (jax.ShapeDtypeStruct((tok_rows, model_width), f32),)
        + (jax.ShapeDtypeStruct((tok_rows, model_width), bf16),) * 3,
        "vvv",
        (4 * lanes * 4 * tok_rows * model_width, 2 << 20),
    )(returned, gates_high, gates_low)
    moe_out = own_part
    for k, part in zip((1, 2, 3), parts):
        moe_out = moe_out + turned(part, "z4", -k).astype(f32)
    layer_out = (mid_states + moe_out).astype(jnp.bfloat16)
    final_normed = layer_norm(layer_out.astype(jnp.float32), gain_rows[2]).astype(jnp.bfloat16)
    teacher = jax.nn.log_softmax(
        jnp.dot(final_normed, shortlist[0], preferred_element_type=jnp.float32), axis=-1
    )
    learner = jax.nn.log_softmax(student[0], axis=-1)
    picked = (targets[0][:, None] == jnp.arange(student.shape[2])).astype(jnp.float32)
    token_loss = jnp.sum(jnp.exp(teacher) * (teacher - learner), axis=-1) - jnp.sum(
        picked * learner, axis=-1
    )
    counted = jnp.where(decoder, is_valid.astype(jnp.float32), 0.0)
    totals = jnp.stack([jnp.sum(token_loss * counted), jnp.sum(counted)])
    for axes in (("x", "zl"), ("y", "core", "z4")):
        count = math.prod(lax.axis_size(a) for a in axes)
        spread_out = jnp.broadcast_to(jnp.pad(totals, (0, 126))[None], (count, 128))
        totals = lax.all_to_all(spread_out, axes, split_axis=0, concat_axis=0, tiled=True).sum(0)[:2]
    return (layer_out[None], totals[0] / totals[1])


def solution(mesh):
    segments, expert_devices = mesh.devices.shape
    experts = 4
    fine = Mesh(
        mesh.devices.reshape(segments // 2, 2, experts, expert_devices // experts // ZL, ZL),
        ("y", "core", "x", "z4", "zl"),
    )
    seg, exp = ("y", "core"), ("x", "z4", "zl")
    placed = (
        P(seg, exp, None),
        P(seg, exp, None),
        P(seg, exp),
        P(seg, exp),
        P(seg, exp, None),
        P(seg, None, None),
        P(seg, None, None),
        P(seg, None, exp),
        P(seg, exp, None),
        P(seg, None, None),
        P(seg, exp, None),
        P(seg, exp),
    )
    return jax.shard_map(
        local,
        mesh=fine,
        in_specs=placed,
        out_specs=(P(seg, exp, None), P()),
        check_vma=False,
    )
```

```python
import functools
import math

import jax
import jax.numpy as jnp
from jax import lax
from jax.experimental import pallas as pl
from jax.experimental.pallas import tpu as pltpu
from jax.sharding import Mesh, PartitionSpec as P

HEADS = 16
HEAD_DIM = 128
LEN = 32
ZL = 4


epsilon = 1e-05
f32, bf16 = jnp.float32, jnp.bfloat16


def passed_along(block, axis, distance):
    devices = range(lax.axis_size(axis))
    route = [(i - distance, i) for i in devices if i - distance in devices]
    return lax.ppermute(block, axis, route)


def turned(block, axis, distance):
    count = math.prod(lax.axis_size(a) for a in ([axis] if isinstance(axis, str) else axis))
    return lax.ppermute(block, axis, [(i, (i + distance) % count) for i in range(count)])


def layer_norm(values, gain_row):
    centred = values - jnp.mean(values, axis=-1, keepdims=True)
    spread = jnp.mean(centred * centred, axis=-1, keepdims=True)
    return centred * lax.rsqrt(spread + epsilon) * gain_row


def kernel_call(body, out_shape, in_specs, cost, limit=40 << 20):
    whole = pl.BlockSpec(memory_space=pltpu.VMEM)
    scalar = pl.BlockSpec(memory_space=pltpu.SMEM)
    return pl.pallas_call(
        body,
        out_shape=out_shape,
        in_specs=[scalar if k == "s" else whole for k in in_specs],
        out_specs=jax.tree.map(lambda _: whole, out_shape),
        cost_estimate=pl.CostEstimate(flops=cost[0], bytes_accessed=cost[1], transcendentals=0),
        compiler_params=pltpu.CompilerParams(vmem_limit_bytes=limit),
    )


def share_body(core, w_in, w_out, out, sems):
    width, hidden = w_in.shape
    half, deep = hidden // 2, width // 2

    def carried(pairs):
        copies = [
            pltpu.make_async_copy(src, dst, sems.at[k]) for k, (src, dst) in enumerate(pairs)
        ]
        for copy in copies:
            copy.start()
        for copy in copies:
            copy.wait()

    @pl.when(core[0] == 0)
    def _():
        carried(
            [
                (
                    w_in.at[pl.ds(d * deep, deep), pl.ds(h * half, half)],
                    out.at[h, :, pl.ds(d * half, half)],
                )
                for h in range(2)
                for d in range(2)
            ]
        )

    @pl.when(core[0] != 0)
    def _():
        carried(
            [
                (
                    w_out.at[pl.ds(h * half, half), pl.ds(p * hidden, hidden)],
                    out.at[h, pl.ds(p * half, half), :],
                )
                for h in range(2)
                for p in range(width // hidden)
            ]
        )


def mlp_body(
    core, rows, w_in, w_out, up0, dn0, fu0, fd0, up1, dn1, fu1, fd1, out,
    own_in, own_out, near_in, near_out, far_in, far_out, act, sems,
):
    width, hidden = w_in.shape
    half, deep = hidden // 2, width // 2
    copy = pltpu.make_async_copy
    first_in = copy(w_in, own_in, sems.at[0])
    first_out = copy(w_out, own_out, sems.at[1])

    def pieces(a, b):
        ins = [
            copy(a[0], near_in.at[0], sems.at[2]),
            copy(a[1], near_in.at[1], sems.at[3]),
            copy(a[2], far_in.at[0], sems.at[4]),
            copy(a[3], far_in.at[1], sems.at[5]),
        ]
        outs = [
            copy(b[0], near_out.at[0], sems.at[6]),
            copy(b[1], near_out.at[1], sems.at[7]),
            copy(b[2], far_out.at[0], sems.at[8]),
            copy(b[3], far_out.at[1], sems.at[9]),
        ]
        return ins, outs

    mine, other = (up0, dn0, fu0, fd0), (up1, dn1, fu1, fd1)
    first_in.start()

    @pl.when(core[0] == 0)
    def _():
        ins, outs = pieces(mine, other)
        for c in ins:
            c.start()
        first_out.start()
        for c in outs:
            c.start()

    @pl.when(core[0] != 0)
    def _():
        ins, outs = pieces(other, mine)
        for c in ins:
            c.start()
        first_out.start()
        for c in outs:
            c.start()

    ins, outs = pieces(mine, other)

    def hidden_of(product):
        return jnp.maximum(product, 0.0).astype(bf16)

    first_in.wait()
    act[:, :hidden] = hidden_of(jnp.dot(rows[...], own_in[...], preferred_element_type=f32))
    pairs = (
        (near_in.at[0, 0], near_in.at[0, 1], near_out.at[0, 0], near_out.at[0, 1]),
        (near_in.at[1, 0], near_in.at[1, 1], near_out.at[1, 0], near_out.at[1, 1]),
        (far_in.at[0], far_in.at[1], far_out.at[0], far_out.at[1]),
    )
    for k, (in_a, in_b, _, _) in enumerate(pairs):
        for c in ins[k : k + 1] if k < 2 else ins[2:]:
            c.wait()
        low = jnp.concatenate([in_a[:, :half], in_b[:, :half]], axis=1)
        high = jnp.concatenate([in_a[:, half:], in_b[:, half:]], axis=1)
        act[:, (k + 1) * hidden : (k + 2) * hidden] = hidden_of(
            jnp.dot(rows[:, :deep], low, preferred_element_type=f32)
            + jnp.dot(rows[:, deep:], high, preferred_element_type=f32)
        )
    first_out.wait()
    for c in outs:
        c.wait()
    for p in range(width // hidden):
        at = slice(p * half, (p + 1) * half)
        cols = slice(p * hidden, (p + 1) * hidden)
        panel = jnp.concatenate(
            [own_out[:, cols]] + [o[at, :] for pair in pairs for o in pair[2:]], axis=0
        )
        out[:, cols] = jnp.dot(act[...], panel, preferred_element_type=f32).astype(bf16)


def normed_of(values, gain):
    centred = values - jnp.mean(values, axis=-1, keepdims=True)
    spread = jnp.mean(centred * centred, axis=-1, keepdims=True)
    return centred * lax.rsqrt(spread + epsilon) * gain


def before_body(facts, hidden, memory, gains, router, routes, mid, block):
    rows, width = hidden.shape
    states = hidden[...].astype(f32)
    queries = normed_of(states, gains[0:1, :]).astype(bf16)
    keys = memory[...]
    heads = [slice(h * HEAD_DIM, (h + 1) * HEAD_DIM) for h in range(HEADS)]
    scores = jnp.concatenate(
        [
            lax.dot_general(
                queries[:, h], keys[:, h], (((1,), (1,)), ((), ())), preferred_element_type=f32
            )
            for h in heads
        ],
        axis=0,
    ) * (1.0 / math.sqrt(HEAD_DIM))
    key_at = lax.broadcasted_iota(jnp.int32, scores.shape, 1)
    scores = jnp.where(key_at < facts[1], scores, -1e30)
    raised = jnp.exp(scores - jnp.max(scores, axis=-1, keepdims=True))
    weights = (raised / jnp.sum(raised, axis=-1, keepdims=True)).astype(bf16)
    attended = jnp.concatenate(
        [
            jnp.dot(weights[i * rows : (i + 1) * rows], keys[:, h], preferred_element_type=f32)
            for i, h in enumerate(heads)
        ],
        axis=1,
    )
    middle = states + jnp.where(facts[2] > 0, attended, 0.0)
    mid[...] = middle
    normed = normed_of(middle, gains[1:2, :]).astype(bf16)
    block[:, :width] = normed
    logits = lax.dot_general(
        normed, router[...], (((1,), (1,)), ((), ())), preferred_element_type=f32
    )
    lane = lax.broadcasted_iota(jnp.int32, logits.shape, 1)
    expert = lane % 8
    real = (expert < 4) & (lane < 16)
    logits = jnp.where(real, logits, -jnp.inf)
    raised = jnp.exp(logits - jnp.max(logits, axis=-1, keepdims=True))
    probs = raised / (0.5 * jnp.sum(raised, axis=-1, keepdims=True))
    first = jnp.where(real & (expert == routes[:, 0:1]), 1.0, 0.0)
    second = jnp.where(real & (expert == routes[:, 1:2]), 1.0, 0.0)
    prob_first = 0.5 * jnp.sum(probs * first, axis=-1, keepdims=True)
    prob_second = 0.5 * jnp.sum(probs * second, axis=-1, keepdims=True)
    gates = (prob_first * first + prob_second * second) / (prob_first + prob_second)
    token = lax.broadcasted_iota(jnp.int32, gates.shape, 0)
    gates = jnp.where(token < facts[0], gates, 0.0)
    upper = gates.astype(bf16).astype(f32)
    block[:, width:] = jnp.where(lane < 8, upper, gates - upper).astype(bf16)


def pack_body(slots, own, b1, b2, b3, rows, high, low):
    width = rows.shape[1]
    lanes = rows.shape[0]
    tokens = jnp.concatenate([own[...], b1[...], b2[...], b3[...]], axis=0)
    count = tokens.shape[0]
    aux = tokens[:, width:]
    lane = lax.broadcasted_iota(jnp.int32, (128, lanes), 1)
    part = lax.broadcasted_iota(jnp.int32, (128, lanes), 0)
    of_expert = lane // slots
    pick_high = (part == of_expert).astype(f32).astype(bf16)
    pick_low = (part == of_expert + 8).astype(f32).astype(bf16)
    gate_high = jnp.dot(aux, pick_high, preferred_element_type=f32)
    gate_low = jnp.dot(aux, pick_low, preferred_element_type=f32)
    chosen = gate_high > 0.0
    upto = (
        lax.broadcasted_iota(jnp.int32, (count, count), 0)
        >= lax.broadcasted_iota(jnp.int32, (count, count), 1)
    ).astype(f32).astype(bf16)
    rank = jnp.dot(upto, chosen.astype(f32).astype(bf16), preferred_element_type=f32)
    slot = (lax.broadcasted_iota(jnp.int32, (count, lanes), 1) % slots + 1).astype(f32)
    here = jnp.where(chosen & (rank == slot), 1.0, 0.0)
    rows[...] = lax.dot_general(
        here.astype(bf16), tokens[:, :width], (((0,), (0,)), ((), ())), preferred_element_type=f32
    ).astype(bf16)
    high[...] = (here * gate_high).astype(bf16)
    low[...] = (here * gate_low).astype(bf16)


def combine_body(rows, high, low, own, o1, o2, o3):
    value = jnp.dot(high[...], rows[...], preferred_element_type=f32) + jnp.dot(
        low[...], rows[...], preferred_element_type=f32
    )
    n = own.shape[0]
    own[...] = value[:n]
    for k, o in enumerate((o1, o2, o3)):
        o[...] = value[(k + 1) * n : (k + 2) * n].astype(bf16)


def local(
    hidden,
    memory,
    lengths,
    memory_lengths,
    routes,
    norm_gain,
    router,
    w_in,
    w_out,
    shortlist,
    student,
    targets,
):
    chips = lax.axis_size("y")
    experts = router.shape[2]
    tok_rows = hidden.shape[1]
    model_width = hidden.shape[2]
    capacity = 5 * tok_rows // 8
    decoder = lax.axis_index("y") >= chips // 2
    is_valid = jnp.arange(tok_rows) < lengths[0, 0]
    arrived, arrived_length = passed_along((memory[0], memory_lengths[0]), "y", chips // 2)
    core = lax.axis_index("core").astype(jnp.int32)[None]
    model_hidden = w_in.shape[2]
    gain_rows = norm_gain[0]
    router_rows = jnp.pad(router[0].T, ((0, 8 - experts), (0, 0)))
    router_rows = jnp.pad(jnp.concatenate([router_rows, router_rows], axis=0), ((0, 112), (0, 0)))
    whole = pl.BlockSpec(memory_space=pltpu.VMEM)
    scalars = pl.BlockSpec(memory_space=pltpu.SMEM)
    anywhere = pl.BlockSpec(memory_space=pl.ANY)
    shared = pl.pallas_call(
        share_body,
        out_shape=jax.ShapeDtypeStruct((2, model_width // 2, model_hidden), bf16),
        in_specs=[scalars] + [anywhere] * 2,
        out_specs=anywhere,
        scratch_shapes=[pltpu.SemaphoreType.DMA((2 * model_width // model_hidden,))],
        cost_estimate=pl.CostEstimate(flops=0, bytes_accessed=2 << 20, transcendentals=0),
    )(core, w_in[0], w_out[0])
    line = ("z4", "zl")
    up, down = turned(shared, line, -1), turned(shared, line, 1)
    far_up, far_down = turned(up[0], line, -1), turned(down[1], line, 1)
    mine = (up, down, far_up, far_down)
    other = [turned(piece, "core", 1) for piece in mine]
    facts = jnp.stack([lengths[0, 0], arrived_length[0], decoder.astype(jnp.int32)])
    mid_states, block = kernel_call(
        before_body,
        (
            jax.ShapeDtypeStruct((tok_rows, model_width), f32),
            jax.ShapeDtypeStruct((tok_rows, model_width + 128), bf16),
        ),
        "svvvvv",
        (4 * tok_rows * LEN * model_width, 1 << 20),
    )(facts, hidden[0], arrived, gain_rows, router_rows, routes[0])
    order = (1, 3, 2)
    visitors = [turned(block, "z4", k) for k in order]
    slots = 4 * capacity
    lanes = experts * slots
    packed, gates_high, gates_low = kernel_call(
        functools.partial(pack_body, slots),
        (
            jax.ShapeDtypeStruct((lanes, model_width), bf16),
            jax.ShapeDtypeStruct((4 * tok_rows, lanes), bf16),
            jax.ShapeDtypeStruct((4 * tok_rows, lanes), bf16),
        ),
        "vvvv",
        (2 * lanes * 4 * tok_rows * model_width, 2 << 20),
    )(block, *visitors)
    rows = lax.all_to_all(packed, "x", split_axis=0, concat_axis=0, tiled=True)
    deep, near = model_width // 2, (2, 2, model_width // 2, model_hidden)
    partial_out = pl.pallas_call(
        mlp_body,
        out_shape=jax.ShapeDtypeStruct((lanes, model_width), bf16),
        in_specs=[scalars, whole] + [anywhere] * 10,
        out_specs=whole,
        scratch_shapes=[
            pltpu.VMEM((model_width, model_hidden), bf16),
            pltpu.VMEM((model_hidden, model_width), bf16),
            pltpu.VMEM(near, bf16),
            pltpu.VMEM(near, bf16),
            pltpu.VMEM((2, deep, model_hidden), bf16),
            pltpu.VMEM((2, deep, model_hidden), bf16),
            pltpu.VMEM((lanes, 4 * model_hidden), bf16),
            pltpu.SemaphoreType.DMA((10,)),
        ],
        cost_estimate=pl.CostEstimate(
            flops=16 * lanes * model_width * model_hidden, bytes_accessed=11 << 20, transcendentals=0
        ),
        compiler_params=pltpu.CompilerParams(vmem_limit_bytes=40 << 20),
    )(core, rows, w_in[0], w_out[0], *mine, *other)
    returned = lax.all_to_all(partial_out, "x", split_axis=0, concat_axis=0, tiled=True)
    own_part, *parts = kernel_call(
        combine_body,
        (jax.ShapeDtypeStruct((tok_rows, model_width), f32),)
        + (jax.ShapeDtypeStruct((tok_rows, model_width), bf16),) * 3,
        "vvv",
        (4 * lanes * 4 * tok_rows * model_width, 2 << 20),
    )(returned, gates_high, gates_low)
    moe_out = own_part
    for k, part in zip(order, parts):
        moe_out = moe_out + turned(part, "z4", -k).astype(f32)
    layer_out = (mid_states + moe_out).astype(jnp.bfloat16)
    final_normed = layer_norm(layer_out.astype(jnp.float32), gain_rows[2]).astype(jnp.bfloat16)
    teacher = jax.nn.log_softmax(
        jnp.dot(final_normed, shortlist[0], preferred_element_type=jnp.float32), axis=-1
    )
    learner = jax.nn.log_softmax(student[0], axis=-1)
    picked = (targets[0][:, None] == jnp.arange(student.shape[2])).astype(jnp.float32)
    token_loss = jnp.sum(jnp.exp(teacher) * (teacher - learner), axis=-1) - jnp.sum(
        picked * learner, axis=-1
    )
    counted = jnp.where(decoder, is_valid.astype(jnp.float32), 0.0)
    totals = jnp.stack([jnp.sum(token_loss * counted), jnp.sum(counted)])
    for axes in (("x", "zl"), ("y", "core", "z4")):
        count = math.prod(lax.axis_size(a) for a in axes)
        spread_out = jnp.broadcast_to(jnp.pad(totals, (0, 126))[None], (count, 128))
        totals = lax.all_to_all(spread_out, axes, split_axis=0, concat_axis=0, tiled=True).sum(0)[:2]
    return (layer_out[None], totals[0] / totals[1])


def solution(mesh):
    segments, expert_devices = mesh.devices.shape
    experts = 4
    fine = Mesh(
        mesh.devices.reshape(segments // 2, 2, experts, expert_devices // experts // ZL, ZL),
        ("y", "core", "x", "z4", "zl"),
    )
    seg, exp = ("y", "core"), ("x", "z4", "zl")
    placed = (
        P(seg, exp, None),
        P(seg, exp, None),
        P(seg, exp),
        P(seg, exp),
        P(seg, exp, None),
        P(seg, None, None),
        P(seg, None, None),
        P(seg, None, exp),
        P(seg, exp, None),
        P(seg, None, None),
        P(seg, exp, None),
        P(seg, exp),
    )
    return jax.shard_map(
        local,
        mesh=fine,
        in_specs=placed,
        out_specs=(P(seg, exp, None), P()),
        check_vma=False,
    )
```

```python
import functools
import math

import jax
import jax.numpy as jnp
from jax import lax
from jax.experimental import pallas as pl
from jax.experimental.pallas import tpu as pltpu
from jax.sharding import Mesh, PartitionSpec as P

HEADS = 16
HEAD_DIM = 128
LEN = 32
ZL = 4


epsilon = 1e-05
f32, bf16 = jnp.float32, jnp.bfloat16


def passed_along(block, axis, distance):
    devices = range(lax.axis_size(axis))
    route = [(i - distance, i) for i in devices if i - distance in devices]
    return lax.ppermute(block, axis, route)


def turned(block, axis, distance):
    count = math.prod(lax.axis_size(a) for a in ([axis] if isinstance(axis, str) else axis))
    return lax.ppermute(block, axis, [(i, (i + distance) % count) for i in range(count)])


def layer_norm(values, gain_row):
    centred = values - jnp.mean(values, axis=-1, keepdims=True)
    spread = jnp.mean(centred * centred, axis=-1, keepdims=True)
    return centred * lax.rsqrt(spread + epsilon) * gain_row


def kernel_call(body, out_shape, in_specs, cost, limit=40 << 20):
    whole = pl.BlockSpec(memory_space=pltpu.VMEM)
    scalar = pl.BlockSpec(memory_space=pltpu.SMEM)
    return pl.pallas_call(
        body,
        out_shape=out_shape,
        in_specs=[scalar if k == "s" else whole for k in in_specs],
        out_specs=jax.tree.map(lambda _: whole, out_shape),
        cost_estimate=pl.CostEstimate(flops=cost[0], bytes_accessed=cost[1], transcendentals=0),
        compiler_params=pltpu.CompilerParams(vmem_limit_bytes=limit),
    )


def share_body(core, w_in, w_out, out, block_in, block_out, sem):
    width, hidden = w_in.shape
    half, deep = hidden // 2, width // 2

    @pl.when(core[0] == 0)
    def _():
        copy = pltpu.make_async_copy(w_in, block_in, sem)
        copy.start()
        copy.wait()
        for h in range(2):
            for d in range(2):
                out[h, :, d * half : (d + 1) * half] = block_in[
                    d * deep : (d + 1) * deep, h * half : (h + 1) * half
                ]

    @pl.when(core[0] != 0)
    def _():
        copy = pltpu.make_async_copy(w_out, block_out, sem)
        copy.start()
        copy.wait()
        for h in range(2):
            for p in range(width // hidden):
                out[h, p * half : (p + 1) * half, :] = block_out[
                    h * half : (h + 1) * half, p * hidden : (p + 1) * hidden
                ]


def mlp_body(
    core, rows, w_in, w_out, up0, dn0, fu0, fd0, up1, dn1, fu1, fd1, out,
    own_in, own_out, near_in, near_out, far_in, far_out, act, sems,
):
    width, hidden = w_in.shape
    half, deep = hidden // 2, width // 2
    copy = pltpu.make_async_copy
    first_in = copy(w_in, own_in, sems.at[0])
    first_out = copy(w_out, own_out, sems.at[1])

    def pieces(a, b):
        ins = [
            copy(a[0], near_in.at[0], sems.at[2]),
            copy(a[1], near_in.at[1], sems.at[3]),
            copy(a[2], far_in.at[0], sems.at[4]),
            copy(a[3], far_in.at[1], sems.at[5]),
        ]
        outs = [
            copy(b[0], near_out.at[0], sems.at[6]),
            copy(b[1], near_out.at[1], sems.at[7]),
            copy(b[2], far_out.at[0], sems.at[8]),
            copy(b[3], far_out.at[1], sems.at[9]),
        ]
        return ins, outs

    mine, other = (up0, dn0, fu0, fd0), (up1, dn1, fu1, fd1)
    first_in.start()

    @pl.when(core[0] == 0)
    def _():
        ins, outs = pieces(mine, other)
        for c in ins:
            c.start()
        first_out.start()
        for c in outs:
            c.start()

    @pl.when(core[0] != 0)
    def _():
        ins, outs = pieces(other, mine)
        for c in ins:
            c.start()
        first_out.start()
        for c in outs:
            c.start()

    ins, outs = pieces(mine, other)

    def hidden_of(product):
        return jnp.maximum(product, 0.0).astype(bf16)

    first_in.wait()
    act[:, :hidden] = hidden_of(jnp.dot(rows[...], own_in[...], preferred_element_type=f32))
    pairs = (
        (near_in.at[0, 0], near_in.at[0, 1], near_out.at[0, 0], near_out.at[0, 1]),
        (near_in.at[1, 0], near_in.at[1, 1], near_out.at[1, 0], near_out.at[1, 1]),
        (far_in.at[0], far_in.at[1], far_out.at[0], far_out.at[1]),
    )
    for k, (in_a, in_b, _, _) in enumerate(pairs):
        for c in ins[k : k + 1] if k < 2 else ins[2:]:
            c.wait()
        low = jnp.concatenate([in_a[:, :half], in_b[:, :half]], axis=1)
        high = jnp.concatenate([in_a[:, half:], in_b[:, half:]], axis=1)
        act[:, (k + 1) * hidden : (k + 2) * hidden] = hidden_of(
            jnp.dot(rows[:, :deep], low, preferred_element_type=f32)
            + jnp.dot(rows[:, deep:], high, preferred_element_type=f32)
        )
    first_out.wait()
    for c in outs:
        c.wait()
    for p in range(width // hidden):
        at = slice(p * half, (p + 1) * half)
        cols = slice(p * hidden, (p + 1) * hidden)
        panel = jnp.concatenate(
            [own_out[:, cols]] + [o[at, :] for pair in pairs for o in pair[2:]], axis=0
        )
        out[:, cols] = jnp.dot(act[...], panel, preferred_element_type=f32).astype(bf16)


def normed_of(values, gain):
    centred = values - jnp.mean(values, axis=-1, keepdims=True)
    spread = jnp.mean(centred * centred, axis=-1, keepdims=True)
    return centred * lax.rsqrt(spread + epsilon) * gain


def before_body(facts, hidden, memory, gains, router, routes, mid, block):
    rows, width = hidden.shape
    states = hidden[...].astype(f32)
    queries = normed_of(states, gains[0:1, :]).astype(bf16)
    keys = memory[...]
    heads = [slice(h * HEAD_DIM, (h + 1) * HEAD_DIM) for h in range(HEADS)]
    scores = jnp.concatenate(
        [
            lax.dot_general(
                queries[:, h], keys[:, h], (((1,), (1,)), ((), ())), preferred_element_type=f32
            )
            for h in heads
        ],
        axis=0,
    ) * (1.0 / math.sqrt(HEAD_DIM))
    key_at = lax.broadcasted_iota(jnp.int32, scores.shape, 1)
    scores = jnp.where(key_at < facts[1], scores, -1e30)
    raised = jnp.exp(scores - jnp.max(scores, axis=-1, keepdims=True))
    weights = (raised / jnp.sum(raised, axis=-1, keepdims=True)).astype(bf16)
    attended = jnp.concatenate(
        [
            jnp.dot(weights[i * rows : (i + 1) * rows], keys[:, h], preferred_element_type=f32)
            for i, h in enumerate(heads)
        ],
        axis=1,
    )
    middle = states + jnp.where(facts[2] > 0, attended, 0.0)
    mid[...] = middle
    normed = normed_of(middle, gains[1:2, :]).astype(bf16)
    block[:, :width] = normed
    logits = lax.dot_general(
        normed, router[...], (((1,), (1,)), ((), ())), preferred_element_type=f32
    )
    lane = lax.broadcasted_iota(jnp.int32, logits.shape, 1)
    expert = lane % 8
    real = (expert < 4) & (lane < 16)
    logits = jnp.where(real, logits, -jnp.inf)
    raised = jnp.exp(logits - jnp.max(logits, axis=-1, keepdims=True))
    probs = raised / (0.5 * jnp.sum(raised, axis=-1, keepdims=True))
    first = jnp.where(real & (expert == routes[:, 0:1]), 1.0, 0.0)
    second = jnp.where(real & (expert == routes[:, 1:2]), 1.0, 0.0)
    prob_first = 0.5 * jnp.sum(probs * first, axis=-1, keepdims=True)
    prob_second = 0.5 * jnp.sum(probs * second, axis=-1, keepdims=True)
    gates = (prob_first * first + prob_second * second) / (prob_first + prob_second)
    token = lax.broadcasted_iota(jnp.int32, gates.shape, 0)
    gates = jnp.where(token < facts[0], gates, 0.0)
    upper = gates.astype(bf16).astype(f32)
    block[:, width:] = jnp.where(lane < 8, upper, gates - upper).astype(bf16)


def pack_body(slots, own, b1, b2, b3, rows, high, low):
    width = rows.shape[1]
    lanes = rows.shape[0]
    tokens = jnp.concatenate([own[...], b1[...], b2[...], b3[...]], axis=0)
    count = tokens.shape[0]
    aux = tokens[:, width:]
    lane = lax.broadcasted_iota(jnp.int32, (128, lanes), 1)
    part = lax.broadcasted_iota(jnp.int32, (128, lanes), 0)
    of_expert = lane // slots
    pick_high = (part == of_expert).astype(f32).astype(bf16)
    pick_low = (part == of_expert + 8).astype(f32).astype(bf16)
    gate_high = jnp.dot(aux, pick_high, preferred_element_type=f32)
    gate_low = jnp.dot(aux, pick_low, preferred_element_type=f32)
    chosen = gate_high > 0.0
    upto = (
        lax.broadcasted_iota(jnp.int32, (count, count), 0)
        >= lax.broadcasted_iota(jnp.int32, (count, count), 1)
    ).astype(f32).astype(bf16)
    rank = jnp.dot(upto, chosen.astype(f32).astype(bf16), preferred_element_type=f32)
    slot = (lax.broadcasted_iota(jnp.int32, (count, lanes), 1) % slots + 1).astype(f32)
    here = jnp.where(chosen & (rank == slot), 1.0, 0.0)
    rows[...] = lax.dot_general(
        here.astype(bf16), tokens[:, :width], (((0,), (0,)), ((), ())), preferred_element_type=f32
    ).astype(bf16)
    high[...] = (here * gate_high).astype(bf16)
    low[...] = (here * gate_low).astype(bf16)


def combine_body(rows, high, low, own, o1, o2, o3):
    value = jnp.dot(high[...], rows[...], preferred_element_type=f32) + jnp.dot(
        low[...], rows[...], preferred_element_type=f32
    )
    n = own.shape[0]
    own[...] = value[:n]
    for k, o in enumerate((o1, o2, o3)):
        o[...] = value[(k + 1) * n : (k + 2) * n].astype(bf16)


def local(
    hidden,
    memory,
    lengths,
    memory_lengths,
    routes,
    norm_gain,
    router,
    w_in,
    w_out,
    shortlist,
    student,
    targets,
):
    chips = lax.axis_size("y")
    experts = router.shape[2]
    tok_rows = hidden.shape[1]
    model_width = hidden.shape[2]
    capacity = 5 * tok_rows // 8
    decoder = lax.axis_index("y") >= chips // 2
    is_valid = jnp.arange(tok_rows) < lengths[0, 0]
    core = lax.axis_index("core").astype(jnp.int32)[None]
    model_hidden = w_in.shape[2]
    gain_rows = norm_gain[0]
    arrived, arrived_length = passed_along((memory[0], memory_lengths[0]), "y", chips // 2)
    router_rows = jnp.pad(router[0].T, ((0, 8 - experts), (0, 0)))
    router_rows = jnp.pad(jnp.concatenate([router_rows, router_rows], axis=0), ((0, 112), (0, 0)))
    whole = pl.BlockSpec(memory_space=pltpu.VMEM)
    scalars = pl.BlockSpec(memory_space=pltpu.SMEM)
    anywhere = pl.BlockSpec(memory_space=pl.ANY)
    shared = pl.pallas_call(
        share_body,
        out_shape=jax.ShapeDtypeStruct((2, model_width // 2, model_hidden), bf16),
        in_specs=[scalars] + [anywhere] * 2,
        out_specs=whole,
        scratch_shapes=[
            pltpu.VMEM((model_width, model_hidden), bf16),
            pltpu.VMEM((model_hidden, model_width), bf16),
            pltpu.SemaphoreType.DMA,
        ],
        cost_estimate=pl.CostEstimate(flops=0, bytes_accessed=2 << 20, transcendentals=0),
        compiler_params=pltpu.CompilerParams(vmem_limit_bytes=56 << 20),
    )(core, w_in[0], w_out[0])
    line = ("z4", "zl")
    up, down = turned(shared, line, -1), turned(shared, line, 1)
    far_up, far_down = turned(up[0], line, -1), turned(down[1], line, 1)
    mine = (up, down, far_up, far_down)
    other = [turned(piece, "core", 1) for piece in mine]
    facts = jnp.stack([lengths[0, 0], arrived_length[0], decoder.astype(jnp.int32)])
    mid_states, block = kernel_call(
        before_body,
        (
            jax.ShapeDtypeStruct((tok_rows, model_width), f32),
            jax.ShapeDtypeStruct((tok_rows, model_width + 128), bf16),
        ),
        "svvvvv",
        (4 * tok_rows * LEN * model_width, 1 << 20),
    )(facts, hidden[0], arrived, gain_rows, router_rows, routes[0])
    order = (1, 3, 2)
    visitors = [turned(block, "z4", k) for k in order]
    slots = 4 * capacity
    lanes = experts * slots
    packed, gates_high, gates_low = kernel_call(
        functools.partial(pack_body, slots),
        (
            jax.ShapeDtypeStruct((lanes, model_width), bf16),
            jax.ShapeDtypeStruct((4 * tok_rows, lanes), bf16),
            jax.ShapeDtypeStruct((4 * tok_rows, lanes), bf16),
        ),
        "vvvv",
        (2 * lanes * 4 * tok_rows * model_width, 2 << 20),
    )(block, *visitors)
    rows = lax.all_to_all(packed, "x", split_axis=0, concat_axis=0, tiled=True)
    deep, near = model_width // 2, (2, 2, model_width // 2, model_hidden)
    partial_out = pl.pallas_call(
        mlp_body,
        out_shape=jax.ShapeDtypeStruct((lanes, model_width), bf16),
        in_specs=[scalars, whole] + [anywhere] * 10,
        out_specs=whole,
        scratch_shapes=[
            pltpu.VMEM((model_width, model_hidden), bf16),
            pltpu.VMEM((model_hidden, model_width), bf16),
            pltpu.VMEM(near, bf16),
            pltpu.VMEM(near, bf16),
            pltpu.VMEM((2, deep, model_hidden), bf16),
            pltpu.VMEM((2, deep, model_hidden), bf16),
            pltpu.VMEM((lanes, 4 * model_hidden), bf16),
            pltpu.SemaphoreType.DMA((10,)),
        ],
        cost_estimate=pl.CostEstimate(
            flops=16 * lanes * model_width * model_hidden, bytes_accessed=11 << 20, transcendentals=0
        ),
        compiler_params=pltpu.CompilerParams(vmem_limit_bytes=58 << 20),
    )(core, rows, w_in[0], w_out[0], *mine, *other)
    returned = lax.all_to_all(partial_out, "x", split_axis=0, concat_axis=0, tiled=True)
    own_part, *parts = kernel_call(
        combine_body,
        (jax.ShapeDtypeStruct((tok_rows, model_width), f32),)
        + (jax.ShapeDtypeStruct((tok_rows, model_width), bf16),) * 3,
        "vvv",
        (4 * lanes * 4 * tok_rows * model_width, 2 << 20),
    )(returned, gates_high, gates_low)
    moe_out = own_part
    for k, part in zip(order, parts):
        moe_out = moe_out + turned(part, "z4", -k).astype(f32)
    layer_out = (mid_states + moe_out).astype(jnp.bfloat16)
    final_normed = layer_norm(layer_out.astype(jnp.float32), gain_rows[2]).astype(jnp.bfloat16)
    teacher = jax.nn.log_softmax(
        jnp.dot(final_normed, shortlist[0], preferred_element_type=jnp.float32), axis=-1
    )
    learner = jax.nn.log_softmax(student[0], axis=-1)
    picked = (targets[0][:, None] == jnp.arange(student.shape[2])).astype(jnp.float32)
    token_loss = jnp.sum(jnp.exp(teacher) * (teacher - learner), axis=-1) - jnp.sum(
        picked * learner, axis=-1
    )
    counted = jnp.where(decoder, is_valid.astype(jnp.float32), 0.0)
    totals = jnp.stack([jnp.sum(token_loss * counted), jnp.sum(counted)])
    for axes in (("x", "zl"), ("y", "core", "z4")):
        count = math.prod(lax.axis_size(a) for a in axes)
        spread_out = jnp.broadcast_to(jnp.pad(totals, (0, 126))[None], (count, 128))
        totals = lax.all_to_all(spread_out, axes, split_axis=0, concat_axis=0, tiled=True).sum(0)[:2]
    return (layer_out[None], totals[0] / totals[1])


def solution(mesh):
    segments, expert_devices = mesh.devices.shape
    experts = 4
    fine = Mesh(
        mesh.devices.reshape(segments // 2, 2, experts, expert_devices // experts // ZL, ZL),
        ("y", "core", "x", "z4", "zl"),
    )
    seg, exp = ("y", "core"), ("x", "z4", "zl")
    placed = (
        P(seg, exp, None),
        P(seg, exp, None),
        P(seg, exp),
        P(seg, exp),
        P(seg, exp, None),
        P(seg, None, None),
        P(seg, None, None),
        P(seg, None, exp),
        P(seg, exp, None),
        P(seg, None, None),
        P(seg, exp, None),
        P(seg, exp),
    )
    return jax.shard_map(
        local,
        mesh=fine,
        in_specs=placed,
        out_specs=(P(seg, exp, None), P()),
        check_vma=False,
    )
```

```python
import functools
import math

import jax
import jax.numpy as jnp
from jax import lax
from jax.experimental import pallas as pl
from jax.experimental.pallas import tpu as pltpu
from jax.sharding import Mesh, PartitionSpec as P

HEADS = 16
HEAD_DIM = 128
LEN = 32
ZL = 4


epsilon = 1e-05
f32, bf16 = jnp.float32, jnp.bfloat16


def passed_along(block, axis, distance):
    devices = range(lax.axis_size(axis))
    route = [(i - distance, i) for i in devices if i - distance in devices]
    return lax.ppermute(block, axis, route)


def turned(block, axis, distance):
    count = math.prod(lax.axis_size(a) for a in ([axis] if isinstance(axis, str) else axis))
    return lax.ppermute(block, axis, [(i, (i + distance) % count) for i in range(count)])


def layer_norm(values, gain_row):
    centred = values - jnp.mean(values, axis=-1, keepdims=True)
    spread = jnp.mean(centred * centred, axis=-1, keepdims=True)
    return centred * lax.rsqrt(spread + epsilon) * gain_row


def kernel_call(body, out_shape, in_specs, cost, limit=24 << 20):
    whole = pl.BlockSpec(memory_space=pltpu.VMEM)
    scalar = pl.BlockSpec(memory_space=pltpu.SMEM)
    return pl.pallas_call(
        body,
        out_shape=out_shape,
        in_specs=[scalar if k == "s" else whole for k in in_specs],
        out_specs=jax.tree.map(lambda _: whole, out_shape),
        cost_estimate=pl.CostEstimate(flops=cost[0], bytes_accessed=cost[1], transcendentals=0),
        compiler_params=pltpu.CompilerParams(vmem_limit_bytes=limit),
    )


def share_body(w_in, w_out, out, block_in, block_out, sems):
    width, hidden = w_in.shape
    half, deep = hidden // 2, width // 2
    first = pltpu.make_async_copy(w_in, block_in, sems.at[0])
    second = pltpu.make_async_copy(w_out, block_out, sems.at[1])
    first.start()
    second.start()
    first.wait()
    for h in range(2):
        for d in range(2):
            out[h, 0, :, d * half : (d + 1) * half] = block_in[
                d * deep : (d + 1) * deep, h * half : (h + 1) * half
            ]
    second.wait()
    for h in range(2):
        for p in range(width // hidden):
            out[h, 1, p * half : (p + 1) * half, :] = block_out[
                h * half : (h + 1) * half, p * hidden : (p + 1) * hidden
            ]


def relay_body(core, near, after, near_out, out, sem):
    del after, near_out
    copy = pltpu.make_async_copy(near.at[core[0]], out, sem)
    copy.start()
    copy.wait()


def later_body(block, after, out):
    del block, after, out


def mlp_body(
    rows, w_in, w_out, near_a, near_b, far_a, far_b, out, own_in, own_out, near, far, act, sems
):
    width, hidden = w_in.shape
    half, deep = hidden // 2, width // 2
    copy = pltpu.make_async_copy
    first_in = copy(w_in, own_in, sems.at[0])
    first_out = copy(w_out, own_out, sems.at[1])
    others = [
        copy(near_a, near.at[0], sems.at[2]),
        copy(near_b, near.at[1], sems.at[3]),
        copy(far_a, far.at[0], sems.at[4]),
        copy(far_b, far.at[1], sems.at[5]),
    ]
    first_in.start()
    for c in others:
        c.start()
    first_out.start()

    def hidden_of(product):
        return jnp.maximum(product, 0.0).astype(bf16)

    first_in.wait()
    act[:, :hidden] = hidden_of(jnp.dot(rows[...], own_in[...], preferred_element_type=f32))
    pairs = (
        (near.at[0, 0], near.at[0, 1]),
        (near.at[1, 0], near.at[1, 1]),
        (far.at[0], far.at[1]),
    )
    for k, (a, b) in enumerate(pairs):
        for c in others[k : k + 1] if k < 2 else others[2:]:
            c.wait()
        low = jnp.concatenate([a[0, :, :half], b[0, :, :half]], axis=1)
        high = jnp.concatenate([a[0, :, half:], b[0, :, half:]], axis=1)
        act[:, (k + 1) * hidden : (k + 2) * hidden] = hidden_of(
            jnp.dot(rows[:, :deep], low, preferred_element_type=f32)
            + jnp.dot(rows[:, deep:], high, preferred_element_type=f32)
        )
    first_out.wait()
    for p in range(width // hidden):
        at = slice(p * half, (p + 1) * half)
        cols = slice(p * hidden, (p + 1) * hidden)
        panel = jnp.concatenate(
            [own_out[:, cols]] + [o[1, at, :] for pair in pairs for o in pair], axis=0
        )
        out[:, cols] = jnp.dot(act[...], panel, preferred_element_type=f32).astype(bf16)


def normed_of(values, gain):
    centred = values - jnp.mean(values, axis=-1, keepdims=True)
    spread = jnp.mean(centred * centred, axis=-1, keepdims=True)
    return centred * lax.rsqrt(spread + epsilon) * gain


def before_body(facts, hidden, memory, gains, router, routes, mid, block):
    rows, width = hidden.shape
    states = hidden[...].astype(f32)
    queries = normed_of(states, gains[0:1, :]).astype(bf16)
    keys = memory[...]
    heads = [slice(h * HEAD_DIM, (h + 1) * HEAD_DIM) for h in range(HEADS)]
    scores = jnp.concatenate(
        [
            lax.dot_general(
                queries[:, h], keys[:, h], (((1,), (1,)), ((), ())), preferred_element_type=f32
            )
            for h in heads
        ],
        axis=0,
    ) * (1.0 / math.sqrt(HEAD_DIM))
    key_at = lax.broadcasted_iota(jnp.int32, scores.shape, 1)
    scores = jnp.where(key_at < facts[1], scores, -1e30)
    raised = jnp.exp(scores - jnp.max(scores, axis=-1, keepdims=True))
    weights = (raised / jnp.sum(raised, axis=-1, keepdims=True)).astype(bf16)
    attended = jnp.concatenate(
        [
            jnp.dot(weights[i * rows : (i + 1) * rows], keys[:, h], preferred_element_type=f32)
            for i, h in enumerate(heads)
        ],
        axis=1,
    )
    middle = states + jnp.where(facts[2] > 0, attended, 0.0)
    mid[...] = middle
    normed = normed_of(middle, gains[1:2, :]).astype(bf16)
    block[:, :width] = normed
    logits = lax.dot_general(
        normed, router[...], (((1,), (1,)), ((), ())), preferred_element_type=f32
    )
    lane = lax.broadcasted_iota(jnp.int32, logits.shape, 1)
    expert = lane % 8
    real = (expert < 4) & (lane < 16)
    logits = jnp.where(real, logits, -jnp.inf)
    raised = jnp.exp(logits - jnp.max(logits, axis=-1, keepdims=True))
    probs = raised / (0.5 * jnp.sum(raised, axis=-1, keepdims=True))
    first = jnp.where(real & (expert == routes[:, 0:1]), 1.0, 0.0)
    second = jnp.where(real & (expert == routes[:, 1:2]), 1.0, 0.0)
    prob_first = 0.5 * jnp.sum(probs * first, axis=-1, keepdims=True)
    prob_second = 0.5 * jnp.sum(probs * second, axis=-1, keepdims=True)
    gates = (prob_first * first + prob_second * second) / (prob_first + prob_second)
    token = lax.broadcasted_iota(jnp.int32, gates.shape, 0)
    gates = jnp.where(token < facts[0], gates, 0.0)
    upper = gates.astype(bf16).astype(f32)
    block[:, width:] = jnp.where(lane < 8, upper, gates - upper).astype(bf16)


def pack_body(slots, own, b1, b2, b3, rows, high, low):
    width = rows.shape[1]
    lanes = rows.shape[0]
    tokens = jnp.concatenate([own[...], b1[...], b2[...], b3[...]], axis=0)
    count = tokens.shape[0]
    aux = tokens[:, width:]
    lane = lax.broadcasted_iota(jnp.int32, (128, lanes), 1)
    part = lax.broadcasted_iota(jnp.int32, (128, lanes), 0)
    of_expert = lane // slots
    pick_high = (part == of_expert).astype(f32).astype(bf16)
    pick_low = (part == of_expert + 8).astype(f32).astype(bf16)
    gate_high = jnp.dot(aux, pick_high, preferred_element_type=f32)
    gate_low = jnp.dot(aux, pick_low, preferred_element_type=f32)
    chosen = gate_high > 0.0
    upto = (
        lax.broadcasted_iota(jnp.int32, (count, count), 0)
        >= lax.broadcasted_iota(jnp.int32, (count, count), 1)
    ).astype(f32).astype(bf16)
    rank = jnp.dot(upto, chosen.astype(f32).astype(bf16), preferred_element_type=f32)
    slot = (lax.broadcasted_iota(jnp.int32, (count, lanes), 1) % slots + 1).astype(f32)
    here = jnp.where(chosen & (rank == slot), 1.0, 0.0)
    rows[...] = lax.dot_general(
        here.astype(bf16), tokens[:, :width], (((0,), (0,)), ((), ())), preferred_element_type=f32
    ).astype(bf16)
    high[...] = (here * gate_high).astype(bf16)
    low[...] = (here * gate_low).astype(bf16)


def combine_body(rows, high, low, own, o1, o2, o3):
    value = jnp.dot(high[...], rows[...], preferred_element_type=f32) + jnp.dot(
        low[...], rows[...], preferred_element_type=f32
    )
    n = own.shape[0]
    own[...] = value[:n]
    for k, o in enumerate((o1, o2, o3)):
        o[...] = value[(k + 1) * n : (k + 2) * n].astype(bf16)


def local(
    hidden,
    memory,
    lengths,
    memory_lengths,
    routes,
    norm_gain,
    router,
    w_in,
    w_out,
    shortlist,
    student,
    targets,
):
    chips = lax.axis_size("y")
    experts = router.shape[2]
    tok_rows = hidden.shape[1]
    model_width = hidden.shape[2]
    capacity = 5 * tok_rows // 8
    decoder = lax.axis_index("y") >= chips // 2
    is_valid = jnp.arange(tok_rows) < lengths[0, 0]
    core = lax.axis_index("core").astype(jnp.int32)[None]
    model_hidden = w_in.shape[2]
    gain_rows = norm_gain[0]
    arrived, arrived_length = passed_along((memory[0], memory_lengths[0]), "y", chips // 2)
    router_rows = jnp.pad(router[0].T, ((0, 8 - experts), (0, 0)))
    router_rows = jnp.pad(jnp.concatenate([router_rows, router_rows], axis=0), ((0, 112), (0, 0)))
    whole = pl.BlockSpec(memory_space=pltpu.VMEM)
    scalars = pl.BlockSpec(memory_space=pltpu.SMEM)
    anywhere = pl.BlockSpec(memory_space=pl.ANY)
    piece = (2, model_width // 2, model_hidden)
    shared = pl.pallas_call(
        share_body,
        out_shape=jax.ShapeDtypeStruct((2,) + piece, bf16),
        in_specs=[anywhere] * 2,
        out_specs=whole,
        scratch_shapes=[
            pltpu.VMEM((model_width, model_hidden), bf16),
            pltpu.VMEM((model_hidden, model_width), bf16),
            pltpu.SemaphoreType.DMA((2,)),
        ],
        cost_estimate=pl.CostEstimate(flops=0, bytes_accessed=4 << 20, transcendentals=0),
        compiler_params=pltpu.CompilerParams(vmem_limit_bytes=56 << 20),
    )(w_in[0], w_out[0])
    line = lax.axis_size("z4") * lax.axis_size("zl")
    onward = [(i, (i - 1) % line) for i in range(line)] + [
        (line + i, line + (i + 1) % line) for i in range(line)
    ]
    facts = jnp.stack([lengths[0, 0], arrived_length[0], decoder.astype(jnp.int32)])
    mid_states, block = kernel_call(
        before_body,
        (
            jax.ShapeDtypeStruct((tok_rows, model_width), f32),
            jax.ShapeDtypeStruct((tok_rows, model_width + 128), bf16),
        ),
        "svvvvv",
        (4 * tok_rows * LEN * model_width, 1 << 20),
    )(facts, hidden[0], arrived, gain_rows, router_rows, routes[0])
    order = (1, 3, 2)
    visitors = [turned(block, "z4", k) for k in order]
    near_mine = lax.ppermute(shared, ("core", "z4", "zl"), onward)
    slots = 4 * capacity
    lanes = experts * slots
    packed, gates_high, gates_low = kernel_call(
        functools.partial(pack_body, slots),
        (
            jax.ShapeDtypeStruct((lanes, model_width), bf16),
            jax.ShapeDtypeStruct((4 * tok_rows, lanes), bf16),
            jax.ShapeDtypeStruct((4 * tok_rows, lanes), bf16),
        ),
        "vvvv",
        (2 * lanes * 4 * tok_rows * model_width, 2 << 20),
    )(block, *visitors)
    near_mine, relayed = pl.pallas_call(
        relay_body,
        out_shape=(
            jax.ShapeDtypeStruct((2,) + piece, bf16),
            jax.ShapeDtypeStruct(piece, bf16),
        ),
        in_specs=[scalars] + [anywhere] * 2,
        out_specs=(anywhere, whole),
        scratch_shapes=[pltpu.SemaphoreType.DMA],
        input_output_aliases={1: 0},
        cost_estimate=pl.CostEstimate(flops=0, bytes_accessed=2 << 20, transcendentals=0),
        compiler_params=pltpu.CompilerParams(vmem_limit_bytes=8 << 20),
    )(core, near_mine, gates_high)
    far_mine = lax.ppermute(relayed, ("core", "z4", "zl"), onward)
    near_other = turned(near_mine, "core", 1)
    rows = lax.all_to_all(packed, "x", split_axis=0, concat_axis=0, tiled=True)
    far_mine = pl.pallas_call(
        later_body,
        out_shape=jax.ShapeDtypeStruct(piece, bf16),
        in_specs=[anywhere] * 2,
        out_specs=anywhere,
        input_output_aliases={0: 0},
        cost_estimate=pl.CostEstimate(flops=0, bytes_accessed=0, transcendentals=0),
        compiler_params=pltpu.CompilerParams(vmem_limit_bytes=4 << 20),
    )(far_mine, rows)
    far_other = turned(far_mine, "core", 1)
    partial_out = pl.pallas_call(
        mlp_body,
        out_shape=jax.ShapeDtypeStruct((lanes, model_width), bf16),
        in_specs=[whole] + [anywhere] * 6,
        out_specs=whole,
        scratch_shapes=[
            pltpu.VMEM((model_width, model_hidden), bf16),
            pltpu.VMEM((model_hidden, model_width), bf16),
            pltpu.VMEM((2, 2) + piece, bf16),
            pltpu.VMEM((2,) + piece, bf16),
            pltpu.VMEM((lanes, 4 * model_hidden), bf16),
            pltpu.SemaphoreType.DMA((6,)),
        ],
        cost_estimate=pl.CostEstimate(
            flops=16 * lanes * model_width * model_hidden, bytes_accessed=11 << 20, transcendentals=0
        ),
        compiler_params=pltpu.CompilerParams(vmem_limit_bytes=58 << 20),
    )(rows, w_in[0], w_out[0], near_mine, near_other, far_mine, far_other)
    returned = lax.all_to_all(partial_out, "x", split_axis=0, concat_axis=0, tiled=True)
    own_part, *parts = kernel_call(
        combine_body,
        (jax.ShapeDtypeStruct((tok_rows, model_width), f32),)
        + (jax.ShapeDtypeStruct((tok_rows, model_width), bf16),) * 3,
        "vvv",
        (4 * lanes * 4 * tok_rows * model_width, 2 << 20),
    )(returned, gates_high, gates_low)
    moe_out = own_part
    for k, part in zip(order, parts):
        moe_out = moe_out + turned(part, "z4", -k).astype(f32)
    layer_out = (mid_states + moe_out).astype(jnp.bfloat16)
    final_normed = layer_norm(layer_out.astype(jnp.float32), gain_rows[2]).astype(jnp.bfloat16)
    teacher = jax.nn.log_softmax(
        jnp.dot(final_normed, shortlist[0], preferred_element_type=jnp.float32), axis=-1
    )
    learner = jax.nn.log_softmax(student[0], axis=-1)
    picked = (targets[0][:, None] == jnp.arange(student.shape[2])).astype(jnp.float32)
    token_loss = jnp.sum(jnp.exp(teacher) * (teacher - learner), axis=-1) - jnp.sum(
        picked * learner, axis=-1
    )
    counted = jnp.where(decoder, is_valid.astype(jnp.float32), 0.0)
    totals = jnp.stack([jnp.sum(token_loss * counted), jnp.sum(counted)])
    for axes in (("x", "zl"), ("y", "core", "z4")):
        count = math.prod(lax.axis_size(a) for a in axes)
        spread_out = jnp.broadcast_to(jnp.pad(totals, (0, 126))[None], (count, 128))
        totals = lax.all_to_all(spread_out, axes, split_axis=0, concat_axis=0, tiled=True).sum(0)[:2]
    return (layer_out[None], totals[0] / totals[1])


def solution(mesh):
    segments, expert_devices = mesh.devices.shape
    experts = 4
    fine = Mesh(
        mesh.devices.reshape(segments // 2, 2, experts, expert_devices // experts // ZL, ZL),
        ("y", "core", "x", "z4", "zl"),
    )
    seg, exp = ("y", "core"), ("x", "z4", "zl")
    placed = (
        P(seg, exp, None),
        P(seg, exp, None),
        P(seg, exp),
        P(seg, exp),
        P(seg, exp, None),
        P(seg, None, None),
        P(seg, None, None),
        P(seg, None, exp),
        P(seg, exp, None),
        P(seg, None, None),
        P(seg, exp, None),
        P(seg, exp),
    )
    return jax.shard_map(
        local,
        mesh=fine,
        in_specs=placed,
        out_specs=(P(seg, exp, None), P()),
        check_vma=False,
    )
```

```python
import functools
import math

import jax
import jax.numpy as jnp
from jax import lax
from jax.experimental import pallas as pl
from jax.experimental.pallas import tpu as pltpu
from jax.sharding import Mesh, PartitionSpec as P

HEADS = 16
HEAD_DIM = 128
LEN = 32
ZL = 4


epsilon = 1e-05
f32, bf16 = jnp.float32, jnp.bfloat16


def passed_along(block, axis, distance):
    devices = range(lax.axis_size(axis))
    route = [(i - distance, i) for i in devices if i - distance in devices]
    return lax.ppermute(block, axis, route)


def turned(block, axis, distance):
    count = math.prod(lax.axis_size(a) for a in ([axis] if isinstance(axis, str) else axis))
    return lax.ppermute(block, axis, [(i, (i + distance) % count) for i in range(count)])


def layer_norm(values, gain_row):
    centred = values - jnp.mean(values, axis=-1, keepdims=True)
    spread = jnp.mean(centred * centred, axis=-1, keepdims=True)
    return centred * lax.rsqrt(spread + epsilon) * gain_row


def kernel_call(body, out_shape, in_specs, cost, limit=24 << 20):
    whole = pl.BlockSpec(memory_space=pltpu.VMEM)
    scalar = pl.BlockSpec(memory_space=pltpu.SMEM)
    return pl.pallas_call(
        body,
        out_shape=out_shape,
        in_specs=[scalar if k == "s" else whole for k in in_specs],
        out_specs=jax.tree.map(lambda _: whole, out_shape),
        cost_estimate=pl.CostEstimate(flops=cost[0], bytes_accessed=cost[1], transcendentals=0),
        compiler_params=pltpu.CompilerParams(vmem_limit_bytes=limit),
    )


def share_body(w_in, w_out, out, block_in, block_out, sems):
    width, hidden = w_in.shape
    half, deep = hidden // 2, width // 2
    first = pltpu.make_async_copy(w_in, block_in, sems.at[0])
    second = pltpu.make_async_copy(w_out, block_out, sems.at[1])
    first.start()
    second.start()
    first.wait()
    for h in range(2):
        for d in range(2):
            out[h, 0, :, d * half : (d + 1) * half] = block_in[
                d * deep : (d + 1) * deep, h * half : (h + 1) * half
            ]
    second.wait()
    for h in range(2):
        for p in range(width // hidden):
            out[h, 1, p * half : (p + 1) * half, :] = block_out[
                h * half : (h + 1) * half, p * hidden : (p + 1) * hidden
            ]


def relay_body(core, near, after, near_out, out, sem):
    del after, near_out
    copy = pltpu.make_async_copy(near.at[core[0]], out, sem)
    copy.start()
    copy.wait()


def later_body(block, after, out):
    del block, after, out


def mlp_body(rows, own, near_a, near_b, far_a, far_b, out, act):
    half = own.shape[3] // 2
    deep = own.shape[2]
    hidden = 2 * half
    pairs = (
        (own.at[0], own.at[1]),
        (near_a.at[0], near_a.at[1]),
        (near_b.at[0], near_b.at[1]),
        (far_a, far_b),
    )
    for k, (a, b) in enumerate(pairs):
        low = jnp.concatenate([a[0, :, :half], b[0, :, :half]], axis=1)
        high = jnp.concatenate([a[0, :, half:], b[0, :, half:]], axis=1)
        product = jnp.dot(rows[:, :deep], low, preferred_element_type=f32) + jnp.dot(
            rows[:, deep:], high, preferred_element_type=f32
        )
        act[:, k * hidden : (k + 1) * hidden] = jnp.maximum(product, 0.0).astype(bf16)
    for p in range(2 * deep // hidden):
        at = slice(p * half, (p + 1) * half)
        panel = jnp.concatenate([o[1, at, :] for pair in pairs for o in pair], axis=0)
        out[:, p * hidden : (p + 1) * hidden] = jnp.dot(
            act[...], panel, preferred_element_type=f32
        ).astype(bf16)


def normed_of(values, gain):
    centred = values - jnp.mean(values, axis=-1, keepdims=True)
    spread = jnp.mean(centred * centred, axis=-1, keepdims=True)
    return centred * lax.rsqrt(spread + epsilon) * gain


def before_body(facts, hidden, memory, gains, router, routes, mid, block):
    rows, width = hidden.shape
    states = hidden[...].astype(f32)
    queries = normed_of(states, gains[0:1, :]).astype(bf16)
    keys = memory[...]
    heads = [slice(h * HEAD_DIM, (h + 1) * HEAD_DIM) for h in range(HEADS)]
    scores = jnp.concatenate(
        [
            lax.dot_general(
                queries[:, h], keys[:, h], (((1,), (1,)), ((), ())), preferred_element_type=f32
            )
            for h in heads
        ],
        axis=0,
    ) * (1.0 / math.sqrt(HEAD_DIM))
    key_at = lax.broadcasted_iota(jnp.int32, scores.shape, 1)
    scores = jnp.where(key_at < facts[1], scores, -1e30)
    raised = jnp.exp(scores - jnp.max(scores, axis=-1, keepdims=True))
    weights = (raised / jnp.sum(raised, axis=-1, keepdims=True)).astype(bf16)
    attended = jnp.concatenate(
        [
            jnp.dot(weights[i * rows : (i + 1) * rows], keys[:, h], preferred_element_type=f32)
            for i, h in enumerate(heads)
        ],
        axis=1,
    )
    middle = states + jnp.where(facts[2] > 0, attended, 0.0)
    mid[...] = middle
    normed = normed_of(middle, gains[1:2, :]).astype(bf16)
    block[:, :width] = normed
    logits = lax.dot_general(
        normed, router[...], (((1,), (1,)), ((), ())), preferred_element_type=f32
    )
    lane = lax.broadcasted_iota(jnp.int32, logits.shape, 1)
    expert = lane % 8
    real = (expert < 4) & (lane < 16)
    logits = jnp.where(real, logits, -jnp.inf)
    raised = jnp.exp(logits - jnp.max(logits, axis=-1, keepdims=True))
    probs = raised / (0.5 * jnp.sum(raised, axis=-1, keepdims=True))
    first = jnp.where(real & (expert == routes[:, 0:1]), 1.0, 0.0)
    second = jnp.where(real & (expert == routes[:, 1:2]), 1.0, 0.0)
    prob_first = 0.5 * jnp.sum(probs * first, axis=-1, keepdims=True)
    prob_second = 0.5 * jnp.sum(probs * second, axis=-1, keepdims=True)
    gates = (prob_first * first + prob_second * second) / (prob_first + prob_second)
    token = lax.broadcasted_iota(jnp.int32, gates.shape, 0)
    gates = jnp.where(token < facts[0], gates, 0.0)
    upper = gates.astype(bf16).astype(f32)
    block[:, width:] = jnp.where(lane < 8, upper, gates - upper).astype(bf16)


def pack_body(slots, own, b1, b2, b3, rows, high, low):
    width = rows.shape[1]
    lanes = rows.shape[0]
    tokens = jnp.concatenate([own[...], b1[...], b2[...], b3[...]], axis=0)
    count = tokens.shape[0]
    aux = tokens[:, width:]
    lane = lax.broadcasted_iota(jnp.int32, (128, lanes), 1)
    part = lax.broadcasted_iota(jnp.int32, (128, lanes), 0)
    of_expert = lane // slots
    pick_high = (part == of_expert).astype(f32).astype(bf16)
    pick_low = (part == of_expert + 8).astype(f32).astype(bf16)
    gate_high = jnp.dot(aux, pick_high, preferred_element_type=f32)
    gate_low = jnp.dot(aux, pick_low, preferred_element_type=f32)
    chosen = gate_high > 0.0
    upto = (
        lax.broadcasted_iota(jnp.int32, (count, count), 0)
        >= lax.broadcasted_iota(jnp.int32, (count, count), 1)
    ).astype(f32).astype(bf16)
    rank = jnp.dot(upto, chosen.astype(f32).astype(bf16), preferred_element_type=f32)
    slot = (lax.broadcasted_iota(jnp.int32, (count, lanes), 1) % slots + 1).astype(f32)
    here = jnp.where(chosen & (rank == slot), 1.0, 0.0)
    rows[...] = lax.dot_general(
        here.astype(bf16), tokens[:, :width], (((0,), (0,)), ((), ())), preferred_element_type=f32
    ).astype(bf16)
    high[...] = (here * gate_high).astype(bf16)
    low[...] = (here * gate_low).astype(bf16)


def combine_body(rows, high, low, own, o1, o2, o3):
    value = jnp.dot(high[...], rows[...], preferred_element_type=f32) + jnp.dot(
        low[...], rows[...], preferred_element_type=f32
    )
    n = own.shape[0]
    own[...] = value[:n]
    for k, o in enumerate((o1, o2, o3)):
        o[...] = value[(k + 1) * n : (k + 2) * n].astype(bf16)


def local(
    hidden,
    memory,
    lengths,
    memory_lengths,
    routes,
    norm_gain,
    router,
    w_in,
    w_out,
    shortlist,
    student,
    targets,
):
    chips = lax.axis_size("y")
    experts = router.shape[2]
    tok_rows = hidden.shape[1]
    model_width = hidden.shape[2]
    capacity = 5 * tok_rows // 8
    decoder = lax.axis_index("y") >= chips // 2
    is_valid = jnp.arange(tok_rows) < lengths[0, 0]
    core = lax.axis_index("core").astype(jnp.int32)[None]
    model_hidden = w_in.shape[2]
    gain_rows = norm_gain[0]
    arrived, arrived_length = passed_along((memory[0], memory_lengths[0]), "y", chips // 2)
    router_rows = jnp.pad(router[0].T, ((0, 8 - experts), (0, 0)))
    router_rows = jnp.pad(jnp.concatenate([router_rows, router_rows], axis=0), ((0, 112), (0, 0)))
    whole = pl.BlockSpec(memory_space=pltpu.VMEM)
    scalars = pl.BlockSpec(memory_space=pltpu.SMEM)
    anywhere = pl.BlockSpec(memory_space=pl.ANY)
    piece = (2, model_width // 2, model_hidden)
    shared = pl.pallas_call(
        share_body,
        out_shape=jax.ShapeDtypeStruct((2,) + piece, bf16),
        in_specs=[anywhere] * 2,
        out_specs=whole,
        scratch_shapes=[
            pltpu.VMEM((model_width, model_hidden), bf16),
            pltpu.VMEM((model_hidden, model_width), bf16),
            pltpu.SemaphoreType.DMA((2,)),
        ],
        cost_estimate=pl.CostEstimate(flops=0, bytes_accessed=4 << 20, transcendentals=0),
        compiler_params=pltpu.CompilerParams(vmem_limit_bytes=56 << 20),
    )(w_in[0], w_out[0])
    line = lax.axis_size("z4") * lax.axis_size("zl")
    onward = [(i, (i - 1) % line) for i in range(line)] + [
        (line + i, line + (i + 1) % line) for i in range(line)
    ]
    facts = jnp.stack([lengths[0, 0], arrived_length[0], decoder.astype(jnp.int32)])
    mid_states, block = kernel_call(
        before_body,
        (
            jax.ShapeDtypeStruct((tok_rows, model_width), f32),
            jax.ShapeDtypeStruct((tok_rows, model_width + 128), bf16),
        ),
        "svvvvv",
        (4 * tok_rows * LEN * model_width, 1 << 20),
    )(facts, hidden[0], arrived, gain_rows, router_rows, routes[0])
    order = (1, 3, 2)
    visitors = [turned(block, "z4", k) for k in order]
    near_mine = lax.ppermute(shared, ("core", "z4", "zl"), onward)
    slots = 4 * capacity
    lanes = experts * slots
    packed, gates_high, gates_low = kernel_call(
        functools.partial(pack_body, slots),
        (
            jax.ShapeDtypeStruct((lanes, model_width), bf16),
            jax.ShapeDtypeStruct((4 * tok_rows, lanes), bf16),
            jax.ShapeDtypeStruct((4 * tok_rows, lanes), bf16),
        ),
        "vvvv",
        (2 * lanes * 4 * tok_rows * model_width, 2 << 20),
    )(block, *visitors)
    near_mine, relayed = pl.pallas_call(
        relay_body,
        out_shape=(
            jax.ShapeDtypeStruct((2,) + piece, bf16),
            jax.ShapeDtypeStruct(piece, bf16),
        ),
        in_specs=[scalars] + [anywhere] * 2,
        out_specs=(anywhere, whole),
        scratch_shapes=[pltpu.SemaphoreType.DMA],
        input_output_aliases={1: 0},
        cost_estimate=pl.CostEstimate(flops=0, bytes_accessed=2 << 20, transcendentals=0),
        compiler_params=pltpu.CompilerParams(vmem_limit_bytes=8 << 20),
    )(core, near_mine, gates_high)
    far_mine = lax.ppermute(relayed, ("core", "z4", "zl"), onward)
    near_other = turned(near_mine, "core", 1)
    rows = lax.all_to_all(packed, "x", split_axis=0, concat_axis=0, tiled=True)
    far_mine = pl.pallas_call(
        later_body,
        out_shape=jax.ShapeDtypeStruct(piece, bf16),
        in_specs=[anywhere] * 2,
        out_specs=anywhere,
        input_output_aliases={0: 0},
        cost_estimate=pl.CostEstimate(flops=0, bytes_accessed=0, transcendentals=0),
        compiler_params=pltpu.CompilerParams(vmem_limit_bytes=4 << 20),
    )(far_mine, rows)
    far_other = turned(far_mine, "core", 1)
    partial_out = pl.pallas_call(
        mlp_body,
        out_shape=jax.ShapeDtypeStruct((lanes, model_width), bf16),
        in_specs=[whole] * 6,
        out_specs=whole,
        scratch_shapes=[
            pltpu.VMEM((lanes, 4 * model_hidden), bf16),
        ],
        cost_estimate=pl.CostEstimate(
            flops=16 * lanes * model_width * model_hidden, bytes_accessed=11 << 20, transcendentals=0
        ),
        compiler_params=pltpu.CompilerParams(vmem_limit_bytes=24 << 20),
    )(rows, shared, near_mine, near_other, far_mine, far_other)
    returned = lax.all_to_all(partial_out, "x", split_axis=0, concat_axis=0, tiled=True)
    own_part, *parts = kernel_call(
        combine_body,
        (jax.ShapeDtypeStruct((tok_rows, model_width), f32),)
        + (jax.ShapeDtypeStruct((tok_rows, model_width), bf16),) * 3,
        "vvv",
        (4 * lanes * 4 * tok_rows * model_width, 2 << 20),
    )(returned, gates_high, gates_low)
    moe_out = own_part
    for k, part in zip(order, parts):
        moe_out = moe_out + turned(part, "z4", -k).astype(f32)
    layer_out = (mid_states + moe_out).astype(jnp.bfloat16)
    final_normed = layer_norm(layer_out.astype(jnp.float32), gain_rows[2]).astype(jnp.bfloat16)
    teacher = jax.nn.log_softmax(
        jnp.dot(final_normed, shortlist[0], preferred_element_type=jnp.float32), axis=-1
    )
    learner = jax.nn.log_softmax(student[0], axis=-1)
    picked = (targets[0][:, None] == jnp.arange(student.shape[2])).astype(jnp.float32)
    token_loss = jnp.sum(jnp.exp(teacher) * (teacher - learner), axis=-1) - jnp.sum(
        picked * learner, axis=-1
    )
    counted = jnp.where(decoder, is_valid.astype(jnp.float32), 0.0)
    totals = jnp.stack([jnp.sum(token_loss * counted), jnp.sum(counted)])
    for axes in (("y", "core", "x", "z4", "zl"),):
        count = math.prod(lax.axis_size(a) for a in axes)
        spread_out = jnp.broadcast_to(jnp.pad(totals, (0, 126))[None], (count, 128))
        totals = lax.all_to_all(spread_out, axes, split_axis=0, concat_axis=0, tiled=True).sum(0)[:2]
    return (layer_out[None], totals[0] / totals[1])


def solution(mesh):
    segments, expert_devices = mesh.devices.shape
    experts = 4
    fine = Mesh(
        mesh.devices.reshape(segments // 2, 2, experts, expert_devices // experts // ZL, ZL),
        ("y", "core", "x", "z4", "zl"),
    )
    seg, exp = ("y", "core"), ("x", "z4", "zl")
    placed = (
        P(seg, exp, None),
        P(seg, exp, None),
        P(seg, exp),
        P(seg, exp),
        P(seg, exp, None),
        P(seg, None, None),
        P(seg, None, None),
        P(seg, None, exp),
        P(seg, exp, None),
        P(seg, None, None),
        P(seg, exp, None),
        P(seg, exp),
    )
    return jax.shard_map(
        local,
        mesh=fine,
        in_specs=placed,
        out_specs=(P(seg, exp, None), P()),
        check_vma=False,
    )
```

```python
import functools
import math

import jax
import jax.numpy as jnp
from jax import lax
from jax.experimental import pallas as pl
from jax.experimental.pallas import tpu as pltpu
from jax.sharding import Mesh, PartitionSpec as P

HEADS = 16
HEAD_DIM = 128
LEN = 32
ZL = 4


epsilon = 1e-05
f32, bf16 = jnp.float32, jnp.bfloat16


def passed_along(block, axis, distance):
    devices = range(lax.axis_size(axis))
    route = [(i - distance, i) for i in devices if i - distance in devices]
    return lax.ppermute(block, axis, route)


def turned(block, axis, distance):
    count = math.prod(lax.axis_size(a) for a in ([axis] if isinstance(axis, str) else axis))
    return lax.ppermute(block, axis, [(i, (i + distance) % count) for i in range(count)])


def kernel_call(body, out_shape, in_specs, cost, limit=24 << 20):
    whole = pl.BlockSpec(memory_space=pltpu.VMEM)
    scalar = pl.BlockSpec(memory_space=pltpu.SMEM)
    return pl.pallas_call(
        body,
        out_shape=out_shape,
        in_specs=[scalar if k == "s" else whole for k in in_specs],
        out_specs=jax.tree.map(lambda _: whole, out_shape),
        cost_estimate=pl.CostEstimate(flops=cost[0], bytes_accessed=cost[1], transcendentals=0),
        compiler_params=pltpu.CompilerParams(vmem_limit_bytes=limit),
    )


def share_body(w_in, w_out, out, block_in, block_out, sems):
    width, hidden = w_in.shape
    half, deep = hidden // 2, width // 2
    first = pltpu.make_async_copy(w_in, block_in, sems.at[0])
    second = pltpu.make_async_copy(w_out, block_out, sems.at[1])
    first.start()
    second.start()
    first.wait()
    for h in range(2):
        for d in range(2):
            out[h, 0, :, d * half : (d + 1) * half] = block_in[
                d * deep : (d + 1) * deep, h * half : (h + 1) * half
            ]
    second.wait()
    for h in range(2):
        for p in range(width // hidden):
            out[h, 1, p * half : (p + 1) * half, :] = block_out[
                h * half : (h + 1) * half, p * hidden : (p + 1) * hidden
            ]


def relay_body(core, near, after, near_out, out, sem):
    del after, near_out
    copy = pltpu.make_async_copy(near.at[core[0]], out, sem)
    copy.start()
    copy.wait()


def later_body(block, after, out):
    del block, after, out


def mlp_body(rows, own, near_a, near_b, far_a, far_b, out, act):
    half = own.shape[3] // 2
    deep = own.shape[2]
    hidden = 2 * half
    pairs = (
        (own.at[0], own.at[1]),
        (near_a.at[0], near_a.at[1]),
        (near_b.at[0], near_b.at[1]),
        (far_a, far_b),
    )
    for k, (a, b) in enumerate(pairs):
        low = jnp.concatenate([a[0, :, :half], b[0, :, :half]], axis=1)
        high = jnp.concatenate([a[0, :, half:], b[0, :, half:]], axis=1)
        product = jnp.dot(rows[:, :deep], low, preferred_element_type=f32) + jnp.dot(
            rows[:, deep:], high, preferred_element_type=f32
        )
        act[:, k * hidden : (k + 1) * hidden] = jnp.maximum(product, 0.0).astype(bf16)
    for p in range(2 * deep // hidden):
        at = slice(p * half, (p + 1) * half)
        panel = jnp.concatenate([o[1, at, :] for pair in pairs for o in pair], axis=0)
        out[:, p * hidden : (p + 1) * hidden] = jnp.dot(
            act[...], panel, preferred_element_type=f32
        ).astype(bf16)


def normed_of(values, gain):
    centred = values - jnp.mean(values, axis=-1, keepdims=True)
    spread = jnp.mean(centred * centred, axis=-1, keepdims=True)
    return centred * lax.rsqrt(spread + epsilon) * gain


def before_body(facts, hidden, memory, gains, router, routes, mid, block):
    rows, width = hidden.shape
    states = hidden[...].astype(f32)
    queries = normed_of(states, gains[0:1, :]).astype(bf16)
    keys = memory[...]
    heads = [slice(h * HEAD_DIM, (h + 1) * HEAD_DIM) for h in range(HEADS)]
    scores = jnp.concatenate(
        [
            lax.dot_general(
                queries[:, h], keys[:, h], (((1,), (1,)), ((), ())), preferred_element_type=f32
            )
            for h in heads
        ],
        axis=0,
    ) * (1.0 / math.sqrt(HEAD_DIM))
    key_at = lax.broadcasted_iota(jnp.int32, scores.shape, 1)
    scores = jnp.where(key_at < facts[1], scores, -1e30)
    raised = jnp.exp(scores - jnp.max(scores, axis=-1, keepdims=True))
    weights = (raised / jnp.sum(raised, axis=-1, keepdims=True)).astype(bf16)
    attended = jnp.concatenate(
        [
            jnp.dot(weights[i * rows : (i + 1) * rows], keys[:, h], preferred_element_type=f32)
            for i, h in enumerate(heads)
        ],
        axis=1,
    )
    middle = states + jnp.where(facts[2] > 0, attended, 0.0)
    mid[...] = middle
    normed = normed_of(middle, gains[1:2, :]).astype(bf16)
    block[:, :width] = normed
    logits = lax.dot_general(
        normed, router[...], (((1,), (1,)), ((), ())), preferred_element_type=f32
    )
    lane = lax.broadcasted_iota(jnp.int32, logits.shape, 1)
    expert = lane % 8
    real = (expert < 4) & (lane < 16)
    logits = jnp.where(real, logits, -jnp.inf)
    raised = jnp.exp(logits - jnp.max(logits, axis=-1, keepdims=True))
    probs = raised / (0.5 * jnp.sum(raised, axis=-1, keepdims=True))
    first = jnp.where(real & (expert == routes[:, 0:1]), 1.0, 0.0)
    second = jnp.where(real & (expert == routes[:, 1:2]), 1.0, 0.0)
    prob_first = 0.5 * jnp.sum(probs * first, axis=-1, keepdims=True)
    prob_second = 0.5 * jnp.sum(probs * second, axis=-1, keepdims=True)
    gates = (prob_first * first + prob_second * second) / (prob_first + prob_second)
    token = lax.broadcasted_iota(jnp.int32, gates.shape, 0)
    gates = jnp.where(token < facts[0], gates, 0.0)
    upper = gates.astype(bf16).astype(f32)
    block[:, width:] = jnp.where(lane < 8, upper, gates - upper).astype(bf16)


def pack_body(slots, own, b1, b2, b3, rows, high, low):
    width = rows.shape[1]
    lanes = rows.shape[0]
    tokens = jnp.concatenate([own[...], b1[...], b2[...], b3[...]], axis=0)
    count = tokens.shape[0]
    aux = tokens[:, width:]
    lane = lax.broadcasted_iota(jnp.int32, (128, lanes), 1)
    part = lax.broadcasted_iota(jnp.int32, (128, lanes), 0)
    of_expert = lane // slots
    pick_high = (part == of_expert).astype(f32).astype(bf16)
    pick_low = (part == of_expert + 8).astype(f32).astype(bf16)
    gate_high = jnp.dot(aux, pick_high, preferred_element_type=f32)
    gate_low = jnp.dot(aux, pick_low, preferred_element_type=f32)
    chosen = gate_high > 0.0
    upto = (
        lax.broadcasted_iota(jnp.int32, (count, count), 0)
        >= lax.broadcasted_iota(jnp.int32, (count, count), 1)
    ).astype(f32).astype(bf16)
    rank = jnp.dot(upto, chosen.astype(f32).astype(bf16), preferred_element_type=f32)
    slot = (lax.broadcasted_iota(jnp.int32, (count, lanes), 1) % slots + 1).astype(f32)
    here = jnp.where(chosen & (rank == slot), 1.0, 0.0)
    rows[...] = lax.dot_general(
        here.astype(bf16), tokens[:, :width], (((0,), (0,)), ((), ())), preferred_element_type=f32
    ).astype(bf16)
    high[...] = (here * gate_high).astype(bf16)
    low[...] = (here * gate_low).astype(bf16)


def combine_body(rows, high, low, own, o1, o2, o3):
    value = jnp.dot(high[...], rows[...], preferred_element_type=f32) + jnp.dot(
        low[...], rows[...], preferred_element_type=f32
    )
    n = own.shape[0]
    own[...] = value[:n]
    for k, o in enumerate((o1, o2, o3)):
        o[...] = value[(k + 1) * n : (k + 2) * n].astype(bf16)


def after_body(
    facts, mid, own, p1, p2, p3, gains, shortlist, student, targets, out, totals
):
    def log_softmax(values):
        moved = values - jnp.max(values, axis=-1, keepdims=True)
        return moved - jnp.log(jnp.sum(jnp.exp(moved), axis=-1, keepdims=True))

    value = mid[...] + own[...]
    for p in (p1, p2, p3):
        value = value + p[...].astype(f32)
    layer = value.astype(bf16)
    out[...] = layer
    final = normed_of(layer.astype(f32), gains[2:3, :]).astype(bf16)
    teacher = log_softmax(jnp.dot(final, shortlist[...], preferred_element_type=f32))
    learner = log_softmax(student[...])
    column = lax.broadcasted_iota(jnp.int32, learner.shape, 1)
    picked = jnp.where(column == targets[...], learner, 0.0)
    token_loss = jnp.sum(jnp.exp(teacher) * (teacher - learner), axis=-1, keepdims=True) - jnp.sum(
        picked, axis=-1, keepdims=True
    )
    token = lax.broadcasted_iota(jnp.int32, token_loss.shape, 0)
    counted = (token < facts[0]) & (facts[2] > 0)
    loss_sum = jnp.sum(jnp.where(counted, token_loss, 0.0))
    loss_count = jnp.sum(jnp.where(counted, 1.0, 0.0))
    lane = lax.broadcasted_iota(jnp.int32, totals.shape, 1)
    totals[...] = jnp.where(lane == 0, loss_sum, jnp.where(lane == 1, loss_count, 0.0))


def local(
    hidden,
    memory,
    lengths,
    memory_lengths,
    routes,
    norm_gain,
    router,
    w_in,
    w_out,
    shortlist,
    student,
    targets,
):
    chips = lax.axis_size("y")
    experts = router.shape[2]
    tok_rows = hidden.shape[1]
    model_width = hidden.shape[2]
    capacity = 5 * tok_rows // 8
    decoder = lax.axis_index("y") >= chips // 2
    core = lax.axis_index("core").astype(jnp.int32)[None]
    model_hidden = w_in.shape[2]
    gain_rows = norm_gain[0]
    arrived, arrived_length = passed_along((memory[0], memory_lengths[0]), "y", chips // 2)
    router_rows = jnp.pad(router[0].T, ((0, 8 - experts), (0, 0)))
    router_rows = jnp.pad(jnp.concatenate([router_rows, router_rows], axis=0), ((0, 112), (0, 0)))
    whole = pl.BlockSpec(memory_space=pltpu.VMEM)
    scalars = pl.BlockSpec(memory_space=pltpu.SMEM)
    anywhere = pl.BlockSpec(memory_space=pl.ANY)
    piece = (2, model_width // 2, model_hidden)
    shared = pl.pallas_call(
        share_body,
        out_shape=jax.ShapeDtypeStruct((2,) + piece, bf16),
        in_specs=[anywhere] * 2,
        out_specs=whole,
        scratch_shapes=[
            pltpu.VMEM((model_width, model_hidden), bf16),
            pltpu.VMEM((model_hidden, model_width), bf16),
            pltpu.SemaphoreType.DMA((2,)),
        ],
        cost_estimate=pl.CostEstimate(flops=0, bytes_accessed=4 << 20, transcendentals=0),
        compiler_params=pltpu.CompilerParams(vmem_limit_bytes=56 << 20),
    )(w_in[0], w_out[0])
    line = lax.axis_size("z4") * lax.axis_size("zl")
    onward = [(i, (i - 1) % line) for i in range(line)] + [
        (line + i, line + (i + 1) % line) for i in range(line)
    ]
    facts = jnp.stack([lengths[0, 0], arrived_length[0], decoder.astype(jnp.int32)])
    mid_states, block = kernel_call(
        before_body,
        (
            jax.ShapeDtypeStruct((tok_rows, model_width), f32),
            jax.ShapeDtypeStruct((tok_rows, model_width + 128), bf16),
        ),
        "svvvvv",
        (4 * tok_rows * LEN * model_width, 1 << 20),
    )(facts, hidden[0], arrived, gain_rows, router_rows, routes[0])
    order = (1, 3, 2)
    visitors = [turned(block, "z4", k) for k in order]
    near_mine = lax.ppermute(shared, ("core", "z4", "zl"), onward)
    slots = 4 * capacity
    lanes = experts * slots
    packed, gates_high, gates_low = kernel_call(
        functools.partial(pack_body, slots),
        (
            jax.ShapeDtypeStruct((lanes, model_width), bf16),
            jax.ShapeDtypeStruct((4 * tok_rows, lanes), bf16),
            jax.ShapeDtypeStruct((4 * tok_rows, lanes), bf16),
        ),
        "vvvv",
        (2 * lanes * 4 * tok_rows * model_width, 2 << 20),
    )(block, *visitors)
    near_mine, relayed = pl.pallas_call(
        relay_body,
        out_shape=(
            jax.ShapeDtypeStruct((2,) + piece, bf16),
            jax.ShapeDtypeStruct(piece, bf16),
        ),
        in_specs=[scalars] + [anywhere] * 2,
        out_specs=(anywhere, whole),
        scratch_shapes=[pltpu.SemaphoreType.DMA],
        input_output_aliases={1: 0},
        cost_estimate=pl.CostEstimate(flops=0, bytes_accessed=2 << 20, transcendentals=0),
        compiler_params=pltpu.CompilerParams(vmem_limit_bytes=8 << 20),
    )(core, near_mine, gates_high)
    far_mine = lax.ppermute(relayed, ("core", "z4", "zl"), onward)
    near_other = turned(near_mine, "core", 1)
    rows = lax.all_to_all(packed, "x", split_axis=0, concat_axis=0, tiled=True)
    far_mine = pl.pallas_call(
        later_body,
        out_shape=jax.ShapeDtypeStruct(piece, bf16),
        in_specs=[anywhere] * 2,
        out_specs=anywhere,
        input_output_aliases={0: 0},
        cost_estimate=pl.CostEstimate(flops=0, bytes_accessed=0, transcendentals=0),
        compiler_params=pltpu.CompilerParams(vmem_limit_bytes=4 << 20),
    )(far_mine, rows)
    far_other = turned(far_mine, "core", 1)
    partial_out = pl.pallas_call(
        mlp_body,
        out_shape=jax.ShapeDtypeStruct((lanes, model_width), bf16),
        in_specs=[whole] * 6,
        out_specs=whole,
        scratch_shapes=[
            pltpu.VMEM((lanes, 4 * model_hidden), bf16),
        ],
        cost_estimate=pl.CostEstimate(
            flops=16 * lanes * model_width * model_hidden, bytes_accessed=11 << 20, transcendentals=0
        ),
        compiler_params=pltpu.CompilerParams(vmem_limit_bytes=24 << 20),
    )(rows, shared, near_mine, near_other, far_mine, far_other)
    returned = lax.all_to_all(partial_out, "x", split_axis=0, concat_axis=0, tiled=True)
    own_part, *parts = kernel_call(
        combine_body,
        (jax.ShapeDtypeStruct((tok_rows, model_width), f32),)
        + (jax.ShapeDtypeStruct((tok_rows, model_width), bf16),) * 3,
        "vvv",
        (4 * lanes * 4 * tok_rows * model_width, 2 << 20),
    )(returned, gates_high, gates_low)
    home = [turned(part, "z4", -k) for k, part in zip(order, parts)]
    local_axes, far_axes = ("x", "zl"), ("y", "core", "z4")
    members = [math.prod(lax.axis_size(a) for a in axes) for axes in (local_axes, far_axes)]
    layer_out, totals = kernel_call(
        after_body,
        (
            jax.ShapeDtypeStruct((tok_rows, model_width), bf16),
            jax.ShapeDtypeStruct((members[0], 128), f32),
        ),
        "svvvvvvvvv",
        (2 * tok_rows * model_width * shortlist.shape[2], 4 << 20),
    )(facts, mid_states, own_part, *home, gain_rows, shortlist[0], student[0], targets[0][:, None])
    totals = lax.all_to_all(totals, local_axes, split_axis=0, concat_axis=0, tiled=True).sum(0)
    totals = jnp.broadcast_to(totals[None], (members[1], 128))
    totals = lax.all_to_all(totals, far_axes, split_axis=0, concat_axis=0, tiled=True).sum(0)
    return (layer_out[None], totals[0] / totals[1])


def solution(mesh):
    segments, expert_devices = mesh.devices.shape
    experts = 4
    fine = Mesh(
        mesh.devices.reshape(segments // 2, 2, experts, expert_devices // experts // ZL, ZL),
        ("y", "core", "x", "z4", "zl"),
    )
    seg, exp = ("y", "core"), ("x", "z4", "zl")
    placed = (
        P(seg, exp, None),
        P(seg, exp, None),
        P(seg, exp),
        P(seg, exp),
        P(seg, exp, None),
        P(seg, None, None),
        P(seg, None, None),
        P(seg, None, exp),
        P(seg, exp, None),
        P(seg, None, None),
        P(seg, exp, None),
        P(seg, exp),
    )
    return jax.shard_map(
        local,
        mesh=fine,
        in_specs=placed,
        out_specs=(P(seg, exp, None), P()),
        check_vma=False,
    )
```

```python
import functools
import math

import jax
import jax.numpy as jnp
from jax import lax
from jax.experimental import pallas as pl
from jax.experimental.pallas import tpu as pltpu
from jax.sharding import Mesh, PartitionSpec as P

HEADS = 16
HEAD_DIM = 128
LEN = 32
ZL = 4


epsilon = 1e-05
f32, bf16 = jnp.float32, jnp.bfloat16


def passed_along(block, axis, distance):
    devices = range(lax.axis_size(axis))
    route = [(i - distance, i) for i in devices if i - distance in devices]
    return lax.ppermute(block, axis, route)


def turned(block, axis, distance):
    count = math.prod(lax.axis_size(a) for a in ([axis] if isinstance(axis, str) else axis))
    return lax.ppermute(block, axis, [(i, (i + distance) % count) for i in range(count)])


def kernel_call(body, out_shape, in_specs, cost, limit=24 << 20):
    whole = pl.BlockSpec(memory_space=pltpu.VMEM)
    scalar = pl.BlockSpec(memory_space=pltpu.SMEM)
    return pl.pallas_call(
        body,
        out_shape=out_shape,
        in_specs=[scalar if k == "s" else whole for k in in_specs],
        out_specs=jax.tree.map(lambda _: whole, out_shape),
        cost_estimate=pl.CostEstimate(flops=cost[0], bytes_accessed=cost[1], transcendentals=0),
        compiler_params=pltpu.CompilerParams(vmem_limit_bytes=limit),
    )


def share_body(w_in, w_out, out, block_in, block_out, sems):
    width, hidden = w_in.shape
    half, deep = hidden // 2, width // 2
    first = pltpu.make_async_copy(w_in, block_in, sems.at[0])
    second = pltpu.make_async_copy(w_out, block_out, sems.at[1])
    first.start()
    second.start()
    first.wait()
    for h in range(2):
        for d in range(2):
            out[h, 0, :, d * half : (d + 1) * half] = block_in[
                d * deep : (d + 1) * deep, h * half : (h + 1) * half
            ]
    second.wait()
    for h in range(2):
        for p in range(width // hidden):
            out[h, 1, p * half : (p + 1) * half, :] = block_out[
                h * half : (h + 1) * half, p * hidden : (p + 1) * hidden
            ]


def relay_body(core, near, after, near_out, out, sem):
    del after, near_out
    copy = pltpu.make_async_copy(near.at[core[0]], out, sem)
    copy.start()
    copy.wait()


def later_body(block, after, out):
    del block, after, out


def mlp_body(rows, own, near_a, near_b, far_a, far_b, out, act):
    half = own.shape[3] // 2
    deep = own.shape[2]
    hidden = 2 * half
    pairs = (
        (own.at[0], own.at[1]),
        (near_a.at[0], near_a.at[1]),
        (near_b.at[0], near_b.at[1]),
        (far_a, far_b),
    )
    for k, (a, b) in enumerate(pairs):
        low = jnp.concatenate([a[0, :, :half], b[0, :, :half]], axis=1)
        high = jnp.concatenate([a[0, :, half:], b[0, :, half:]], axis=1)
        product = jnp.dot(rows[:, :deep], low, preferred_element_type=f32) + jnp.dot(
            rows[:, deep:], high, preferred_element_type=f32
        )
        act[:, k * hidden : (k + 1) * hidden] = jnp.maximum(product, 0.0).astype(bf16)
    for p in range(2 * deep // hidden):
        at = slice(p * half, (p + 1) * half)
        panel = jnp.concatenate([o[1, at, :] for pair in pairs for o in pair], axis=0)
        out[:, p * hidden : (p + 1) * hidden] = jnp.dot(
            act[...], panel, preferred_element_type=f32
        ).astype(bf16)


def normed_of(values, gain):
    centred = values - jnp.mean(values, axis=-1, keepdims=True)
    spread = jnp.mean(centred * centred, axis=-1, keepdims=True)
    return centred * lax.rsqrt(spread + epsilon) * gain


def before_body(facts, hidden, memory, gains, router, routes, mid, block):
    rows, width = hidden.shape
    states = hidden[...].astype(f32)
    queries = normed_of(states, gains[0:1, :]).astype(bf16)
    keys = memory[...]
    heads = [slice(h * HEAD_DIM, (h + 1) * HEAD_DIM) for h in range(HEADS)]
    scores = jnp.concatenate(
        [
            lax.dot_general(
                queries[:, h], keys[:, h], (((1,), (1,)), ((), ())), preferred_element_type=f32
            )
            for h in heads
        ],
        axis=0,
    ) * (1.0 / math.sqrt(HEAD_DIM))
    key_at = lax.broadcasted_iota(jnp.int32, scores.shape, 1)
    scores = jnp.where(key_at < facts[1], scores, -1e30)
    raised = jnp.exp(scores - jnp.max(scores, axis=-1, keepdims=True))
    weights = (raised / jnp.sum(raised, axis=-1, keepdims=True)).astype(bf16)
    attended = jnp.concatenate(
        [
            jnp.dot(weights[i * rows : (i + 1) * rows], keys[:, h], preferred_element_type=f32)
            for i, h in enumerate(heads)
        ],
        axis=1,
    )
    middle = states + jnp.where(facts[2] > 0, attended, 0.0)
    mid[...] = middle
    normed = normed_of(middle, gains[1:2, :]).astype(bf16)
    block[:, :width] = normed
    logits = lax.dot_general(
        normed, router[...], (((1,), (1,)), ((), ())), preferred_element_type=f32
    )
    lane = lax.broadcasted_iota(jnp.int32, logits.shape, 1)
    expert = lane % 8
    real = (expert < 4) & (lane < 16)
    logits = jnp.where(real, logits, -jnp.inf)
    raised = jnp.exp(logits - jnp.max(logits, axis=-1, keepdims=True))
    probs = raised / (0.5 * jnp.sum(raised, axis=-1, keepdims=True))
    first = jnp.where(real & (expert == routes[:, 0:1]), 1.0, 0.0)
    second = jnp.where(real & (expert == routes[:, 1:2]), 1.0, 0.0)
    prob_first = 0.5 * jnp.sum(probs * first, axis=-1, keepdims=True)
    prob_second = 0.5 * jnp.sum(probs * second, axis=-1, keepdims=True)
    gates = (prob_first * first + prob_second * second) / (prob_first + prob_second)
    token = lax.broadcasted_iota(jnp.int32, gates.shape, 0)
    gates = jnp.where(token < facts[0], gates, 0.0)
    upper = gates.astype(bf16).astype(f32)
    block[:, width:] = jnp.where(lane < 8, upper, gates - upper).astype(bf16)


def pack_body(slots, own, b1, b2, b3, rows, high, low):
    width = rows.shape[1]
    lanes = rows.shape[0]
    tokens = jnp.concatenate([own[...], b1[...], b2[...], b3[...]], axis=0)
    count = tokens.shape[0]
    aux = tokens[:, width:]
    lane = lax.broadcasted_iota(jnp.int32, (128, lanes), 1)
    part = lax.broadcasted_iota(jnp.int32, (128, lanes), 0)
    of_expert = lane // slots
    pick_high = (part == of_expert).astype(f32).astype(bf16)
    pick_low = (part == of_expert + 8).astype(f32).astype(bf16)
    gate_high = jnp.dot(aux, pick_high, preferred_element_type=f32)
    gate_low = jnp.dot(aux, pick_low, preferred_element_type=f32)
    chosen = gate_high > 0.0
    upto = (
        lax.broadcasted_iota(jnp.int32, (count, count), 0)
        >= lax.broadcasted_iota(jnp.int32, (count, count), 1)
    ).astype(f32).astype(bf16)
    rank = jnp.dot(upto, chosen.astype(f32).astype(bf16), preferred_element_type=f32)
    slot = (lax.broadcasted_iota(jnp.int32, (count, lanes), 1) % slots + 1).astype(f32)
    here = jnp.where(chosen & (rank == slot), 1.0, 0.0)
    rows[...] = lax.dot_general(
        here.astype(bf16), tokens[:, :width], (((0,), (0,)), ((), ())), preferred_element_type=f32
    ).astype(bf16)
    high[...] = (here * gate_high).astype(bf16)
    low[...] = (here * gate_low).astype(bf16)


def combine_body(rows, high, low, own, o1, o2, o3):
    value = jnp.dot(high[...], rows[...], preferred_element_type=f32) + jnp.dot(
        low[...], rows[...], preferred_element_type=f32
    )
    n = own.shape[0]
    own[...] = value[:n]
    for k, o in enumerate((o1, o2, o3)):
        o[...] = value[(k + 1) * n : (k + 2) * n].astype(bf16)


def after_body(
    facts, mid, own, p1, p2, p3, gains, shortlist, student, targets, out, totals
):
    def log_softmax(values):
        moved = values - jnp.max(values, axis=-1, keepdims=True)
        return moved - jnp.log(jnp.sum(jnp.exp(moved), axis=-1, keepdims=True))

    value = mid[...] + own[...]
    for p in (p1, p2, p3):
        value = value + p[...].astype(f32)
    layer = value.astype(bf16)
    out[...] = layer
    final = normed_of(layer.astype(f32), gains[2:3, :]).astype(bf16)
    teacher = log_softmax(jnp.dot(final, shortlist[...], preferred_element_type=f32))
    learner = log_softmax(student[...])
    column = lax.broadcasted_iota(jnp.int32, learner.shape, 1)
    picked = jnp.where(column == targets[...], learner, 0.0)
    token_loss = jnp.sum(jnp.exp(teacher) * (teacher - learner), axis=-1, keepdims=True) - jnp.sum(
        picked, axis=-1, keepdims=True
    )
    token = lax.broadcasted_iota(jnp.int32, token_loss.shape, 0)
    counted = (token < facts[0]) & (facts[2] > 0)
    loss_sum = jnp.sum(jnp.where(counted, token_loss, 0.0))
    loss_count = jnp.sum(jnp.where(counted, 1.0, 0.0))
    lane = lax.broadcasted_iota(jnp.int32, totals.shape, 1)
    totals[...] = jnp.where(lane == 0, loss_sum, jnp.where(lane == 1, loss_count, 0.0))


def local(
    hidden,
    memory,
    lengths,
    memory_lengths,
    routes,
    norm_gain,
    router,
    w_in,
    w_out,
    shortlist,
    student,
    targets,
):
    chips = lax.axis_size("y")
    experts = router.shape[2]
    tok_rows = hidden.shape[1]
    model_width = hidden.shape[2]
    capacity = 5 * tok_rows // 8
    decoder = lax.axis_index("y") >= chips // 2
    core = lax.axis_index("core").astype(jnp.int32)[None]
    model_hidden = w_in.shape[2]
    gain_rows = norm_gain[0]
    arrived, arrived_length = passed_along((memory[0], memory_lengths[0]), "y", chips // 2)
    router_rows = jnp.pad(router[0].T, ((0, 8 - experts), (0, 0)))
    router_rows = jnp.pad(jnp.concatenate([router_rows, router_rows], axis=0), ((0, 112), (0, 0)))
    whole = pl.BlockSpec(memory_space=pltpu.VMEM)
    scalars = pl.BlockSpec(memory_space=pltpu.SMEM)
    anywhere = pl.BlockSpec(memory_space=pl.ANY)
    piece = (2, model_width // 2, model_hidden)
    shared = pl.pallas_call(
        share_body,
        out_shape=jax.ShapeDtypeStruct((2,) + piece, bf16),
        in_specs=[anywhere] * 2,
        out_specs=whole,
        scratch_shapes=[
            pltpu.VMEM((model_width, model_hidden), bf16),
            pltpu.VMEM((model_hidden, model_width), bf16),
            pltpu.SemaphoreType.DMA((2,)),
        ],
        cost_estimate=pl.CostEstimate(flops=0, bytes_accessed=4 << 20, transcendentals=0),
        compiler_params=pltpu.CompilerParams(vmem_limit_bytes=56 << 20),
    )(w_in[0], w_out[0])
    line = lax.axis_size("z4") * lax.axis_size("zl")
    onward = [(i, (i - 1) % line) for i in range(line)] + [
        (line + i, line + (i + 1) % line) for i in range(line)
    ]
    facts = jnp.stack([lengths[0, 0], arrived_length[0], decoder.astype(jnp.int32)])
    mid_states, block = kernel_call(
        before_body,
        (
            jax.ShapeDtypeStruct((tok_rows, model_width), f32),
            jax.ShapeDtypeStruct((tok_rows, model_width + 128), bf16),
        ),
        "svvvvv",
        (4 * tok_rows * LEN * model_width, 1 << 20),
    )(facts, hidden[0], arrived, gain_rows, router_rows, routes[0])
    order = (2, 1, 3)
    visitors = [turned(block, "z4", k) for k in order]
    near_mine = lax.ppermute(shared, ("core", "z4", "zl"), onward)
    slots = 4 * capacity
    lanes = experts * slots
    packed, gates_high, gates_low = kernel_call(
        functools.partial(pack_body, slots),
        (
            jax.ShapeDtypeStruct((lanes, model_width), bf16),
            jax.ShapeDtypeStruct((4 * tok_rows, lanes), bf16),
            jax.ShapeDtypeStruct((4 * tok_rows, lanes), bf16),
        ),
        "vvvv",
        (2 * lanes * 4 * tok_rows * model_width, 2 << 20),
    )(block, *visitors)
    near_mine, relayed = pl.pallas_call(
        relay_body,
        out_shape=(
            jax.ShapeDtypeStruct((2,) + piece, bf16),
            jax.ShapeDtypeStruct(piece, bf16),
        ),
        in_specs=[scalars] + [anywhere] * 2,
        out_specs=(anywhere, whole),
        scratch_shapes=[pltpu.SemaphoreType.DMA],
        input_output_aliases={1: 0},
        cost_estimate=pl.CostEstimate(flops=0, bytes_accessed=2 << 20, transcendentals=0),
        compiler_params=pltpu.CompilerParams(vmem_limit_bytes=8 << 20),
    )(core, near_mine, gates_high)
    far_mine = lax.ppermute(relayed, ("core", "z4", "zl"), onward)
    near_other = turned(near_mine, "core", 1)
    rows = lax.all_to_all(packed, "x", split_axis=0, concat_axis=0, tiled=True)
    far_mine = pl.pallas_call(
        later_body,
        out_shape=jax.ShapeDtypeStruct(piece, bf16),
        in_specs=[anywhere] * 2,
        out_specs=anywhere,
        input_output_aliases={0: 0},
        cost_estimate=pl.CostEstimate(flops=0, bytes_accessed=0, transcendentals=0),
        compiler_params=pltpu.CompilerParams(vmem_limit_bytes=4 << 20),
    )(far_mine, rows)
    far_other = turned(far_mine, "core", 1)
    partial_out = pl.pallas_call(
        mlp_body,
        out_shape=jax.ShapeDtypeStruct((lanes, model_width), bf16),
        in_specs=[whole] * 6,
        out_specs=whole,
        scratch_shapes=[
            pltpu.VMEM((lanes, 4 * model_hidden), bf16),
        ],
        cost_estimate=pl.CostEstimate(
            flops=16 * lanes * model_width * model_hidden, bytes_accessed=11 << 20, transcendentals=0
        ),
        compiler_params=pltpu.CompilerParams(vmem_limit_bytes=24 << 20),
    )(rows, shared, near_mine, near_other, far_mine, far_other)
    returned = lax.all_to_all(partial_out, "x", split_axis=0, concat_axis=0, tiled=True)
    own_part, *parts = kernel_call(
        combine_body,
        (jax.ShapeDtypeStruct((tok_rows, model_width), f32),)
        + (jax.ShapeDtypeStruct((tok_rows, model_width), bf16),) * 3,
        "vvv",
        (4 * lanes * 4 * tok_rows * model_width, 2 << 20),
    )(returned, gates_high, gates_low)
    home = [turned(part, "z4", -k) for k, part in zip(order, parts)]
    local_axes, far_axes = ("x", "zl"), ("y", "core", "z4")
    members = [math.prod(lax.axis_size(a) for a in axes) for axes in (local_axes, far_axes)]
    layer_out, totals = kernel_call(
        after_body,
        (
            jax.ShapeDtypeStruct((tok_rows, model_width), bf16),
            jax.ShapeDtypeStruct((members[0], 128), f32),
        ),
        "svvvvvvvvv",
        (2 * tok_rows * model_width * shortlist.shape[2], 4 << 20),
    )(facts, mid_states, own_part, *home, gain_rows, shortlist[0], student[0], targets[0][:, None])
    totals = lax.all_to_all(totals, local_axes, split_axis=0, concat_axis=0, tiled=True).sum(0)
    totals = jnp.broadcast_to(totals[None], (members[1], 128))
    totals = lax.all_to_all(totals, far_axes, split_axis=0, concat_axis=0, tiled=True).sum(0)
    return (layer_out[None], totals[0] / totals[1])


def solution(mesh):
    segments, expert_devices = mesh.devices.shape
    experts = 4
    fine = Mesh(
        mesh.devices.reshape(segments // 2, 2, experts, expert_devices // experts // ZL, ZL),
        ("y", "core", "x", "z4", "zl"),
    )
    seg, exp = ("y", "core"), ("x", "z4", "zl")
    placed = (
        P(seg, exp, None),
        P(seg, exp, None),
        P(seg, exp),
        P(seg, exp),
        P(seg, exp, None),
        P(seg, None, None),
        P(seg, None, None),
        P(seg, None, exp),
        P(seg, exp, None),
        P(seg, None, None),
        P(seg, exp, None),
        P(seg, exp),
    )
    return jax.shard_map(
        local,
        mesh=fine,
        in_specs=placed,
        out_specs=(P(seg, exp, None), P()),
        check_vma=False,
    )
```

```python
import functools
import math

import jax
import jax.numpy as jnp
from jax import lax
from jax.experimental import pallas as pl
from jax.experimental.pallas import tpu as pltpu
from jax.sharding import Mesh, PartitionSpec as P

HEADS = 16
HEAD_DIM = 128
LEN = 32
ZL = 4


epsilon = 1e-05
f32, bf16 = jnp.float32, jnp.bfloat16


def passed_along(block, axis, distance):
    devices = range(lax.axis_size(axis))
    route = [(i - distance, i) for i in devices if i - distance in devices]
    return lax.ppermute(block, axis, route)


def turned(block, axis, distance):
    count = math.prod(lax.axis_size(a) for a in ([axis] if isinstance(axis, str) else axis))
    return lax.ppermute(block, axis, [(i, (i + distance) % count) for i in range(count)])


def kernel_call(body, out_shape, in_specs, cost, limit=24 << 20):
    whole = pl.BlockSpec(memory_space=pltpu.VMEM)
    scalar = pl.BlockSpec(memory_space=pltpu.SMEM)
    return pl.pallas_call(
        body,
        out_shape=out_shape,
        in_specs=[scalar if k == "s" else whole for k in in_specs],
        out_specs=jax.tree.map(lambda _: whole, out_shape),
        cost_estimate=pl.CostEstimate(flops=cost[0], bytes_accessed=cost[1], transcendentals=0),
        compiler_params=pltpu.CompilerParams(vmem_limit_bytes=limit),
    )


def share_body(w_in, w_out, out, block_in, block_out, sems):
    width, hidden = w_in.shape
    half, deep = hidden // 2, width // 2
    first = pltpu.make_async_copy(w_in, block_in, sems.at[0])
    second = pltpu.make_async_copy(w_out, block_out, sems.at[1])
    first.start()
    second.start()
    first.wait()
    for h in range(2):
        for d in range(2):
            out[h, 0, :, d * half : (d + 1) * half] = block_in[
                d * deep : (d + 1) * deep, h * half : (h + 1) * half
            ]
    second.wait()
    for h in range(2):
        for p in range(width // hidden):
            out[h, 1, p * half : (p + 1) * half, :] = block_out[
                h * half : (h + 1) * half, p * hidden : (p + 1) * hidden
            ]


def relay_body(core, near, after, near_out, out, sem):
    del after, near_out
    copy = pltpu.make_async_copy(near.at[core[0]], out, sem)
    copy.start()
    copy.wait()


def later_body(block, one, two, three, out):
    del block, one, two, three, out


def mlp_body(
    r0, r1, r2, r3, own, near_a, near_b, far_a, far_b, o0, o1, o2, o3, rows, act
):
    slots = r0.shape[0]
    for k, r in enumerate((r0, r1, r2, r3)):
        rows[k * slots : (k + 1) * slots, :] = r[...]
    half = own.shape[3] // 2
    deep = own.shape[2]
    hidden = 2 * half
    pairs = (
        (own.at[0], own.at[1]),
        (near_a.at[0], near_a.at[1]),
        (near_b.at[0], near_b.at[1]),
        (far_a, far_b),
    )
    for k, (a, b) in enumerate(pairs):
        low = jnp.concatenate([a[0, :, :half], b[0, :, :half]], axis=1)
        high = jnp.concatenate([a[0, :, half:], b[0, :, half:]], axis=1)
        product = jnp.dot(rows[:, :deep], low, preferred_element_type=f32) + jnp.dot(
            rows[:, deep:], high, preferred_element_type=f32
        )
        act[:, k * hidden : (k + 1) * hidden] = jnp.maximum(product, 0.0).astype(bf16)
    for p in range(2 * deep // hidden):
        at = slice(p * half, (p + 1) * half)
        panel = jnp.concatenate([o[1, at, :] for pair in pairs for o in pair], axis=0)
        product = jnp.dot(act[...], panel, preferred_element_type=f32).astype(bf16)
        for k, o in enumerate((o0, o1, o2, o3)):
            o[:, p * hidden : (p + 1) * hidden] = product[k * slots : (k + 1) * slots]


def normed_of(values, gain):
    centred = values - jnp.mean(values, axis=-1, keepdims=True)
    spread = jnp.mean(centred * centred, axis=-1, keepdims=True)
    return centred * lax.rsqrt(spread + epsilon) * gain


def before_body(facts, hidden, memory, gains, router, routes, mid, block):
    rows, width = hidden.shape
    states = hidden[...].astype(f32)
    queries = normed_of(states, gains[0:1, :]).astype(bf16)
    keys = memory[...]
    heads = [slice(h * HEAD_DIM, (h + 1) * HEAD_DIM) for h in range(HEADS)]
    scores = jnp.concatenate(
        [
            lax.dot_general(
                queries[:, h], keys[:, h], (((1,), (1,)), ((), ())), preferred_element_type=f32
            )
            for h in heads
        ],
        axis=0,
    ) * (1.0 / math.sqrt(HEAD_DIM))
    key_at = lax.broadcasted_iota(jnp.int32, scores.shape, 1)
    scores = jnp.where(key_at < facts[1], scores, -1e30)
    raised = jnp.exp(scores - jnp.max(scores, axis=-1, keepdims=True))
    weights = (raised / jnp.sum(raised, axis=-1, keepdims=True)).astype(bf16)
    attended = jnp.concatenate(
        [
            jnp.dot(weights[i * rows : (i + 1) * rows], keys[:, h], preferred_element_type=f32)
            for i, h in enumerate(heads)
        ],
        axis=1,
    )
    middle = states + jnp.where(facts[2] > 0, attended, 0.0)
    mid[...] = middle
    normed = normed_of(middle, gains[1:2, :]).astype(bf16)
    block[:, :width] = normed
    logits = lax.dot_general(
        normed, router[...], (((1,), (1,)), ((), ())), preferred_element_type=f32
    )
    lane = lax.broadcasted_iota(jnp.int32, logits.shape, 1)
    expert = lane % 8
    real = (expert < 4) & (lane < 16)
    logits = jnp.where(real, logits, -jnp.inf)
    raised = jnp.exp(logits - jnp.max(logits, axis=-1, keepdims=True))
    probs = raised / (0.5 * jnp.sum(raised, axis=-1, keepdims=True))
    first = jnp.where(real & (expert == routes[:, 0:1]), 1.0, 0.0)
    second = jnp.where(real & (expert == routes[:, 1:2]), 1.0, 0.0)
    prob_first = 0.5 * jnp.sum(probs * first, axis=-1, keepdims=True)
    prob_second = 0.5 * jnp.sum(probs * second, axis=-1, keepdims=True)
    gates = (prob_first * first + prob_second * second) / (prob_first + prob_second)
    token = lax.broadcasted_iota(jnp.int32, gates.shape, 0)
    gates = jnp.where(token < facts[0], gates, 0.0)
    upper = gates.astype(bf16).astype(f32)
    block[:, width:] = jnp.where(lane < 8, upper, gates - upper).astype(bf16)


def pack_body(slots, facts, own, b1, b2, b3, r0, r1, r2, r3, high, low):
    width = r0.shape[1]
    lanes = 4 * slots
    tokens = jnp.concatenate([own[...], b1[...], b2[...], b3[...]], axis=0)
    count = tokens.shape[0]
    aux = tokens[:, width:]
    lane = lax.broadcasted_iota(jnp.int32, (128, lanes), 1)
    part = lax.broadcasted_iota(jnp.int32, (128, lanes), 0)
    of_expert = (lane // slots + facts[3]) % 4
    pick_high = (part == of_expert).astype(f32).astype(bf16)
    pick_low = (part == of_expert + 8).astype(f32).astype(bf16)
    gate_high = jnp.dot(aux, pick_high, preferred_element_type=f32)
    gate_low = jnp.dot(aux, pick_low, preferred_element_type=f32)
    chosen = gate_high > 0.0
    upto = (
        lax.broadcasted_iota(jnp.int32, (count, count), 0)
        >= lax.broadcasted_iota(jnp.int32, (count, count), 1)
    ).astype(f32).astype(bf16)
    rank = jnp.dot(upto, chosen.astype(f32).astype(bf16), preferred_element_type=f32)
    slot = (lax.broadcasted_iota(jnp.int32, (count, lanes), 1) % slots + 1).astype(f32)
    here = jnp.where(chosen & (rank == slot), 1.0, 0.0)
    rows = lax.dot_general(
        here.astype(bf16), tokens[:, :width], (((0,), (0,)), ((), ())), preferred_element_type=f32
    ).astype(bf16)
    for k, r in enumerate((r0, r1, r2, r3)):
        r[...] = rows[k * slots : (k + 1) * slots]
    high[...] = (here * gate_high).astype(bf16)
    low[...] = (here * gate_low).astype(bf16)


def combine_body(r0, r1, r2, r3, high, low, own, o1, o2, o3):
    rows = jnp.concatenate([r0[...], r1[...], r2[...], r3[...]], axis=0)
    value = jnp.dot(high[...], rows, preferred_element_type=f32) + jnp.dot(
        low[...], rows, preferred_element_type=f32
    )
    n = own.shape[0]
    own[...] = value[:n]
    for k, o in enumerate((o1, o2, o3)):
        o[...] = value[(k + 1) * n : (k + 2) * n].astype(bf16)


def after_body(
    facts, mid, own, p1, p2, p3, gains, shortlist, student, targets, out, totals
):
    def log_softmax(values):
        moved = values - jnp.max(values, axis=-1, keepdims=True)
        return moved - jnp.log(jnp.sum(jnp.exp(moved), axis=-1, keepdims=True))

    value = mid[...] + own[...]
    for p in (p1, p2, p3):
        value = value + p[...].astype(f32)
    layer = value.astype(bf16)
    out[...] = layer
    final = normed_of(layer.astype(f32), gains[2:3, :]).astype(bf16)
    teacher = log_softmax(jnp.dot(final, shortlist[...], preferred_element_type=f32))
    learner = log_softmax(student[...])
    column = lax.broadcasted_iota(jnp.int32, learner.shape, 1)
    picked = jnp.where(column == targets[...], learner, 0.0)
    token_loss = jnp.sum(jnp.exp(teacher) * (teacher - learner), axis=-1, keepdims=True) - jnp.sum(
        picked, axis=-1, keepdims=True
    )
    token = lax.broadcasted_iota(jnp.int32, token_loss.shape, 0)
    counted = (token < facts[0]) & (facts[2] > 0)
    loss_sum = jnp.sum(jnp.where(counted, token_loss, 0.0))
    loss_count = jnp.sum(jnp.where(counted, 1.0, 0.0))
    lane = lax.broadcasted_iota(jnp.int32, totals.shape, 1)
    totals[...] = jnp.where(lane == 0, loss_sum, jnp.where(lane == 1, loss_count, 0.0))


def local(
    hidden,
    memory,
    lengths,
    memory_lengths,
    routes,
    norm_gain,
    router,
    w_in,
    w_out,
    shortlist,
    student,
    targets,
):
    chips = lax.axis_size("y")
    experts = router.shape[2]
    tok_rows = hidden.shape[1]
    model_width = hidden.shape[2]
    capacity = 5 * tok_rows // 8
    decoder = lax.axis_index("y") >= chips // 2
    core = lax.axis_index("core").astype(jnp.int32)[None]
    model_hidden = w_in.shape[2]
    gain_rows = norm_gain[0]
    arrived, arrived_length = passed_along((memory[0], memory_lengths[0]), "y", chips // 2)
    router_rows = jnp.pad(router[0].T, ((0, 8 - experts), (0, 0)))
    router_rows = jnp.pad(jnp.concatenate([router_rows, router_rows], axis=0), ((0, 112), (0, 0)))
    whole = pl.BlockSpec(memory_space=pltpu.VMEM)
    scalars = pl.BlockSpec(memory_space=pltpu.SMEM)
    anywhere = pl.BlockSpec(memory_space=pl.ANY)
    piece = (2, model_width // 2, model_hidden)
    shared = pl.pallas_call(
        share_body,
        out_shape=jax.ShapeDtypeStruct((2,) + piece, bf16),
        in_specs=[anywhere] * 2,
        out_specs=whole,
        scratch_shapes=[
            pltpu.VMEM((model_width, model_hidden), bf16),
            pltpu.VMEM((model_hidden, model_width), bf16),
            pltpu.SemaphoreType.DMA((2,)),
        ],
        cost_estimate=pl.CostEstimate(flops=0, bytes_accessed=4 << 20, transcendentals=0),
        compiler_params=pltpu.CompilerParams(vmem_limit_bytes=56 << 20),
    )(w_in[0], w_out[0])
    line = lax.axis_size("z4") * lax.axis_size("zl")
    onward = [(i, (i - 1) % line) for i in range(line)] + [
        (line + i, line + (i + 1) % line) for i in range(line)
    ]
    facts = jnp.stack([lengths[0, 0], arrived_length[0], decoder.astype(jnp.int32),
         lax.axis_index("x").astype(jnp.int32)])
    mid_states, block = kernel_call(
        before_body,
        (
            jax.ShapeDtypeStruct((tok_rows, model_width), f32),
            jax.ShapeDtypeStruct((tok_rows, model_width + 128), bf16),
        ),
        "svvvvv",
        (4 * tok_rows * LEN * model_width, 1 << 20),
    )(facts, hidden[0], arrived, gain_rows, router_rows, routes[0])
    order = (2, 1, 3)
    visitors = [turned(block, "z4", k) for k in order]
    near_mine = lax.ppermute(shared, ("core", "z4", "zl"), onward)
    slots = 4 * capacity
    lanes = experts * slots
    block_shape = jax.ShapeDtypeStruct((slots, model_width), bf16)
    *packed, gates_high, gates_low = kernel_call(
        functools.partial(pack_body, slots),
        (block_shape,) * 4 + (jax.ShapeDtypeStruct((4 * tok_rows, lanes), bf16),) * 2,
        "svvvv",
        (2 * lanes * 4 * tok_rows * model_width, 2 << 20),
    )(facts, block, *visitors)
    across = (2, 1, 3)
    rows = [packed[0], None, None, None]
    for k in across:
        rows[k] = turned(packed[k], "x", k)
    near_mine, relayed = pl.pallas_call(
        relay_body,
        out_shape=(
            jax.ShapeDtypeStruct((2,) + piece, bf16),
            jax.ShapeDtypeStruct(piece, bf16),
        ),
        in_specs=[scalars] + [anywhere] * 2,
        out_specs=(anywhere, whole),
        scratch_shapes=[pltpu.SemaphoreType.DMA],
        input_output_aliases={1: 0},
        cost_estimate=pl.CostEstimate(flops=0, bytes_accessed=2 << 20, transcendentals=0),
        compiler_params=pltpu.CompilerParams(vmem_limit_bytes=8 << 20),
    )(core, near_mine, gates_high)
    far_mine = lax.ppermute(relayed, ("core", "z4", "zl"), onward)
    near_other = turned(near_mine, "core", 1)
    far_mine = pl.pallas_call(
        later_body,
        out_shape=jax.ShapeDtypeStruct(piece, bf16),
        in_specs=[anywhere] * 4,
        out_specs=anywhere,
        input_output_aliases={0: 0},
        cost_estimate=pl.CostEstimate(flops=0, bytes_accessed=0, transcendentals=0),
        compiler_params=pltpu.CompilerParams(vmem_limit_bytes=4 << 20),
    )(far_mine, *rows[1:])
    far_other = turned(far_mine, "core", 1)
    partial_out = pl.pallas_call(
        mlp_body,
        out_shape=(block_shape,) * 4,
        in_specs=[whole] * 9,
        out_specs=(whole,) * 4,
        scratch_shapes=[
            pltpu.VMEM((lanes, model_width), bf16),
            pltpu.VMEM((lanes, 4 * model_hidden), bf16),
        ],
        cost_estimate=pl.CostEstimate(
            flops=16 * lanes * model_width * model_hidden, bytes_accessed=11 << 20, transcendentals=0
        ),
        compiler_params=pltpu.CompilerParams(vmem_limit_bytes=24 << 20),
    )(*rows, shared, near_mine, near_other, far_mine, far_other)
    returned = [partial_out[0], None, None, None]
    for k in across:
        returned[k] = turned(partial_out[k], "x", -k)
    own_part, *parts = kernel_call(
        combine_body,
        (jax.ShapeDtypeStruct((tok_rows, model_width), f32),)
        + (jax.ShapeDtypeStruct((tok_rows, model_width), bf16),) * 3,
        "vvvvvv",
        (4 * lanes * 4 * tok_rows * model_width, 2 << 20),
    )(*returned, gates_high, gates_low)
    home = [turned(part, "z4", -k) for k, part in zip(order, parts)]
    local_axes, far_axes = ("x", "zl"), ("y", "core", "z4")
    members = [math.prod(lax.axis_size(a) for a in axes) for axes in (local_axes, far_axes)]
    layer_out, totals = kernel_call(
        after_body,
        (
            jax.ShapeDtypeStruct((tok_rows, model_width), bf16),
            jax.ShapeDtypeStruct((members[0], 128), f32),
        ),
        "svvvvvvvvv",
        (2 * tok_rows * model_width * shortlist.shape[2], 4 << 20),
    )(facts, mid_states, own_part, *home, gain_rows, shortlist[0], student[0], targets[0][:, None])
    totals = lax.all_to_all(totals, local_axes, split_axis=0, concat_axis=0, tiled=True).sum(0)
    totals = jnp.broadcast_to(totals[None], (members[1], 128))
    totals = lax.all_to_all(totals, far_axes, split_axis=0, concat_axis=0, tiled=True).sum(0)
    return (layer_out[None], totals[0] / totals[1])


def solution(mesh):
    segments, expert_devices = mesh.devices.shape
    experts = 4
    fine = Mesh(
        mesh.devices.reshape(segments // 2, 2, experts, expert_devices // experts // ZL, ZL),
        ("y", "core", "x", "z4", "zl"),
    )
    seg, exp = ("y", "core"), ("x", "z4", "zl")
    placed = (
        P(seg, exp, None),
        P(seg, exp, None),
        P(seg, exp),
        P(seg, exp),
        P(seg, exp, None),
        P(seg, None, None),
        P(seg, None, None),
        P(seg, None, exp),
        P(seg, exp, None),
        P(seg, None, None),
        P(seg, exp, None),
        P(seg, exp),
    )
    return jax.shard_map(
        local,
        mesh=fine,
        in_specs=placed,
        out_specs=(P(seg, exp, None), P()),
        check_vma=False,
    )
```

```python
import functools
import math

import jax
import jax.numpy as jnp
from jax import lax
from jax.experimental import pallas as pl
from jax.experimental.pallas import tpu as pltpu
from jax.sharding import Mesh, PartitionSpec as P

HEADS = 16
HEAD_DIM = 128
LEN = 32
ZL = 4


epsilon = 1e-05
f32, bf16 = jnp.float32, jnp.bfloat16


def passed_along(block, axis, distance):
    devices = range(lax.axis_size(axis))
    route = [(i - distance, i) for i in devices if i - distance in devices]
    return lax.ppermute(block, axis, route)


def turned(block, axis, distance):
    count = math.prod(lax.axis_size(a) for a in ([axis] if isinstance(axis, str) else axis))
    return lax.ppermute(block, axis, [(i, (i + distance) % count) for i in range(count)])


def kernel_call(body, out_shape, in_specs, cost, limit=24 << 20):
    whole = pl.BlockSpec(memory_space=pltpu.VMEM)
    scalar = pl.BlockSpec(memory_space=pltpu.SMEM)
    return pl.pallas_call(
        body,
        out_shape=out_shape,
        in_specs=[scalar if k == "s" else whole for k in in_specs],
        out_specs=jax.tree.map(lambda _: whole, out_shape),
        cost_estimate=pl.CostEstimate(flops=cost[0], bytes_accessed=cost[1], transcendentals=0),
        compiler_params=pltpu.CompilerParams(vmem_limit_bytes=limit),
    )


def share_body(w_in, w_out, out, block_in, block_out, sems):
    width, hidden = w_in.shape
    half, deep = hidden // 2, width // 2
    first = pltpu.make_async_copy(w_in, block_in, sems.at[0])
    second = pltpu.make_async_copy(w_out, block_out, sems.at[1])
    first.start()
    second.start()
    first.wait()
    for h in range(2):
        for d in range(2):
            out[h, 0, :, d * half : (d + 1) * half] = block_in[
                d * deep : (d + 1) * deep, h * half : (h + 1) * half
            ]
    second.wait()
    for h in range(2):
        for p in range(width // hidden):
            out[h, 1, p * half : (p + 1) * half, :] = block_out[
                h * half : (h + 1) * half, p * hidden : (p + 1) * hidden
            ]


def relay_body(core, near, after, near_out, out, sem):
    del after, near_out
    copy = pltpu.make_async_copy(near.at[core[0]], out, sem)
    copy.start()
    copy.wait()


def mlp_body(rows, own, near_a, near_b, far_a, far_b, out, act):
    half = own.shape[3] // 2
    deep = own.shape[2]
    hidden = 2 * half
    pairs = (
        (own.at[0], own.at[1]),
        (near_a.at[0], near_a.at[1]),
        (near_b.at[0], near_b.at[1]),
        (far_a, far_b),
    )
    for k, (a, b) in enumerate(pairs):
        low = jnp.concatenate([a[0, :, :half], b[0, :, :half]], axis=1)
        high = jnp.concatenate([a[0, :, half:], b[0, :, half:]], axis=1)
        product = jnp.dot(rows[:, :deep], low, preferred_element_type=f32) + jnp.dot(
            rows[:, deep:], high, preferred_element_type=f32
        )
        act[:, k * hidden : (k + 1) * hidden] = jnp.maximum(product, 0.0).astype(bf16)
    for p in range(2 * deep // hidden):
        at = slice(p * half, (p + 1) * half)
        panel = jnp.concatenate([o[1, at, :] for pair in pairs for o in pair], axis=0)
        out[:, p * hidden : (p + 1) * hidden] = jnp.dot(
            act[...], panel, preferred_element_type=f32
        ).astype(bf16)


def normed_of(values, gain):
    centred = values - jnp.mean(values, axis=-1, keepdims=True)
    spread = jnp.mean(centred * centred, axis=-1, keepdims=True)
    return centred * lax.rsqrt(spread + epsilon) * gain


def before_body(facts, hidden, memory, gains, router, routes, mid, block):
    rows, width = hidden.shape
    states = hidden[...].astype(f32)
    queries = normed_of(states, gains[0:1, :]).astype(bf16)
    keys = memory[...]
    heads = [slice(h * HEAD_DIM, (h + 1) * HEAD_DIM) for h in range(HEADS)]
    scores = jnp.concatenate(
        [
            lax.dot_general(
                queries[:, h], keys[:, h], (((1,), (1,)), ((), ())), preferred_element_type=f32
            )
            for h in heads
        ],
        axis=0,
    ) * (1.0 / math.sqrt(HEAD_DIM))
    key_at = lax.broadcasted_iota(jnp.int32, scores.shape, 1)
    scores = jnp.where(key_at < facts[1], scores, -1e30)
    raised = jnp.exp(scores - jnp.max(scores, axis=-1, keepdims=True))
    weights = (raised / jnp.sum(raised, axis=-1, keepdims=True)).astype(bf16)
    attended = jnp.concatenate(
        [
            jnp.dot(weights[i * rows : (i + 1) * rows], keys[:, h], preferred_element_type=f32)
            for i, h in enumerate(heads)
        ],
        axis=1,
    )
    middle = states + jnp.where(facts[2] > 0, attended, 0.0)
    mid[...] = middle
    normed = normed_of(middle, gains[1:2, :]).astype(bf16)
    block[:, :width] = normed
    logits = lax.dot_general(
        normed, router[...], (((1,), (1,)), ((), ())), preferred_element_type=f32
    )
    lane = lax.broadcasted_iota(jnp.int32, logits.shape, 1)
    expert = lane % 8
    real = (expert < 4) & (lane < 16)
    logits = jnp.where(real, logits, -jnp.inf)
    raised = jnp.exp(logits - jnp.max(logits, axis=-1, keepdims=True))
    probs = raised / (0.5 * jnp.sum(raised, axis=-1, keepdims=True))
    first = jnp.where(real & (expert == routes[:, 0:1]), 1.0, 0.0)
    second = jnp.where(real & (expert == routes[:, 1:2]), 1.0, 0.0)
    prob_first = 0.5 * jnp.sum(probs * first, axis=-1, keepdims=True)
    prob_second = 0.5 * jnp.sum(probs * second, axis=-1, keepdims=True)
    gates = (prob_first * first + prob_second * second) / (prob_first + prob_second)
    token = lax.broadcasted_iota(jnp.int32, gates.shape, 0)
    gates = jnp.where(token < facts[0], gates, 0.0)
    upper = gates.astype(bf16).astype(f32)
    block[:, width:] = jnp.where(lane < 8, upper, gates - upper).astype(bf16)


def pack_body(slots, own, b1, b2, b3, rows, high, low):
    width = rows.shape[1]
    lanes = rows.shape[0]
    tokens = jnp.concatenate([own[...], b1[...], b2[...], b3[...]], axis=0)
    count = tokens.shape[0]
    aux = tokens[:, width:]
    lane = lax.broadcasted_iota(jnp.int32, (128, lanes), 1)
    part = lax.broadcasted_iota(jnp.int32, (128, lanes), 0)
    of_expert = lane // slots
    pick_high = (part == of_expert).astype(f32).astype(bf16)
    pick_low = (part == of_expert + 8).astype(f32).astype(bf16)
    gate_high = jnp.dot(aux, pick_high, preferred_element_type=f32)
    gate_low = jnp.dot(aux, pick_low, preferred_element_type=f32)
    chosen = gate_high > 0.0
    upto = (
        lax.broadcasted_iota(jnp.int32, (count, count), 0)
        >= lax.broadcasted_iota(jnp.int32, (count, count), 1)
    ).astype(f32).astype(bf16)
    rank = jnp.dot(upto, chosen.astype(f32).astype(bf16), preferred_element_type=f32)
    slot = (lax.broadcasted_iota(jnp.int32, (count, lanes), 1) % slots + 1).astype(f32)
    here = jnp.where(chosen & (rank == slot), 1.0, 0.0)
    rows[...] = lax.dot_general(
        here.astype(bf16), tokens[:, :width], (((0,), (0,)), ((), ())), preferred_element_type=f32
    ).astype(bf16)
    high[...] = (here * gate_high).astype(bf16)
    low[...] = (here * gate_low).astype(bf16)


def combine_body(rows, high, low, own, o1, o2, o3):
    value = jnp.dot(high[...], rows[...], preferred_element_type=f32) + jnp.dot(
        low[...], rows[...], preferred_element_type=f32
    )
    n = own.shape[0]
    own[...] = value[:n]
    for k, o in enumerate((o1, o2, o3)):
        o[...] = value[(k + 1) * n : (k + 2) * n].astype(bf16)


def after_body(
    facts, mid, own, p1, p2, p3, gains, shortlist, student, targets, out, totals
):
    def log_softmax(values):
        moved = values - jnp.max(values, axis=-1, keepdims=True)
        return moved - jnp.log(jnp.sum(jnp.exp(moved), axis=-1, keepdims=True))

    value = mid[...] + own[...]
    for p in (p1, p2, p3):
        value = value + p[...].astype(f32)
    layer = value.astype(bf16)
    out[...] = layer
    final = normed_of(layer.astype(f32), gains[2:3, :]).astype(bf16)
    teacher = log_softmax(jnp.dot(final, shortlist[...], preferred_element_type=f32))
    learner = log_softmax(student[...])
    column = lax.broadcasted_iota(jnp.int32, learner.shape, 1)
    picked = jnp.where(column == targets[...], learner, 0.0)
    token_loss = jnp.sum(jnp.exp(teacher) * (teacher - learner), axis=-1, keepdims=True) - jnp.sum(
        picked, axis=-1, keepdims=True
    )
    token = lax.broadcasted_iota(jnp.int32, token_loss.shape, 0)
    counted = (token < facts[0]) & (facts[2] > 0)
    loss_sum = jnp.sum(jnp.where(counted, token_loss, 0.0))
    loss_count = jnp.sum(jnp.where(counted, 1.0, 0.0))
    lane = lax.broadcasted_iota(jnp.int32, totals.shape, 1)
    totals[...] = jnp.where(lane == 0, loss_sum, jnp.where(lane == 1, loss_count, 0.0))


def local(
    hidden,
    memory,
    lengths,
    memory_lengths,
    routes,
    norm_gain,
    router,
    w_in,
    w_out,
    shortlist,
    student,
    targets,
):
    chips = lax.axis_size("y")
    experts = router.shape[2]
    tok_rows = hidden.shape[1]
    model_width = hidden.shape[2]
    capacity = 5 * tok_rows // 8
    decoder = lax.axis_index("y") >= chips // 2
    core = lax.axis_index("core").astype(jnp.int32)[None]
    model_hidden = w_in.shape[2]
    gain_rows = norm_gain[0]
    arrived, arrived_length = passed_along((memory[0], memory_lengths[0]), "y", chips // 2)
    router_rows = jnp.pad(router[0].T, ((0, 8 - experts), (0, 0)))
    router_rows = jnp.pad(jnp.concatenate([router_rows, router_rows], axis=0), ((0, 112), (0, 0)))
    whole = pl.BlockSpec(memory_space=pltpu.VMEM)
    scalars = pl.BlockSpec(memory_space=pltpu.SMEM)
    anywhere = pl.BlockSpec(memory_space=pl.ANY)
    piece = (2, model_width // 2, model_hidden)
    shared = pl.pallas_call(
        share_body,
        out_shape=jax.ShapeDtypeStruct((2,) + piece, bf16),
        in_specs=[anywhere] * 2,
        out_specs=whole,
        scratch_shapes=[
            pltpu.VMEM((model_width, model_hidden), bf16),
            pltpu.VMEM((model_hidden, model_width), bf16),
            pltpu.SemaphoreType.DMA((2,)),
        ],
        cost_estimate=pl.CostEstimate(flops=0, bytes_accessed=4 << 20, transcendentals=0),
        compiler_params=pltpu.CompilerParams(vmem_limit_bytes=56 << 20),
    )(w_in[0], w_out[0])
    line = lax.axis_size("z4") * lax.axis_size("zl")
    onward = [(i, (i - 1) % line) for i in range(line)] + [
        (line + i, line + (i + 1) % line) for i in range(line)
    ]
    facts = jnp.stack([lengths[0, 0], arrived_length[0], decoder.astype(jnp.int32)])
    mid_states, block = kernel_call(
        before_body,
        (
            jax.ShapeDtypeStruct((tok_rows, model_width), f32),
            jax.ShapeDtypeStruct((tok_rows, model_width + 128), bf16),
        ),
        "svvvvv",
        (4 * tok_rows * LEN * model_width, 1 << 20),
    )(facts, hidden[0], arrived, gain_rows, router_rows, routes[0])
    order = (2, 1, 3)
    visitors = [turned(block, "z4", k) for k in order]
    near_mine = lax.ppermute(shared, ("core", "z4", "zl"), onward)
    slots = 4 * capacity
    lanes = experts * slots
    packed, gates_high, gates_low = kernel_call(
        functools.partial(pack_body, slots),
        (
            jax.ShapeDtypeStruct((lanes, model_width), bf16),
            jax.ShapeDtypeStruct((4 * tok_rows, lanes), bf16),
            jax.ShapeDtypeStruct((4 * tok_rows, lanes), bf16),
        ),
        "vvvv",
        (2 * lanes * 4 * tok_rows * model_width, 2 << 20),
    )(block, *visitors)
    near_mine, relayed = pl.pallas_call(
        relay_body,
        out_shape=(
            jax.ShapeDtypeStruct((2,) + piece, bf16),
            jax.ShapeDtypeStruct(piece, bf16),
        ),
        in_specs=[scalars] + [anywhere] * 2,
        out_specs=(anywhere, whole),
        scratch_shapes=[pltpu.SemaphoreType.DMA],
        input_output_aliases={1: 0},
        cost_estimate=pl.CostEstimate(flops=0, bytes_accessed=2 << 20, transcendentals=0),
        compiler_params=pltpu.CompilerParams(vmem_limit_bytes=8 << 20),
    )(core, near_mine, gates_high)
    far_mine = lax.ppermute(relayed, ("core", "z4", "zl"), onward)
    crossing = [(i, (j + line) % (2 * line)) for i, j in onward]
    far_other = lax.ppermute(relayed, ("core", "z4", "zl"), crossing)
    near_other = turned(near_mine, "core", 1)
    rows = lax.all_to_all(packed, "x", split_axis=0, concat_axis=0, tiled=True)
    partial_out = pl.pallas_call(
        mlp_body,
        out_shape=jax.ShapeDtypeStruct((lanes, model_width), bf16),
        in_specs=[whole] * 6,
        out_specs=whole,
        scratch_shapes=[
            pltpu.VMEM((lanes, 4 * model_hidden), bf16),
        ],
        cost_estimate=pl.CostEstimate(
            flops=16 * lanes * model_width * model_hidden, bytes_accessed=11 << 20, transcendentals=0
        ),
        compiler_params=pltpu.CompilerParams(vmem_limit_bytes=24 << 20),
    )(rows, shared, near_mine, near_other, far_mine, far_other)
    returned = lax.all_to_all(partial_out, "x", split_axis=0, concat_axis=0, tiled=True)
    own_part, *parts = kernel_call(
        combine_body,
        (jax.ShapeDtypeStruct((tok_rows, model_width), f32),)
        + (jax.ShapeDtypeStruct((tok_rows, model_width), bf16),) * 3,
        "vvv",
        (4 * lanes * 4 * tok_rows * model_width, 2 << 20),
    )(returned, gates_high, gates_low)
    home = [turned(part, "z4", -k) for k, part in zip(order, parts)]
    local_axes, far_axes = ("x", "zl"), ("y", "core", "z4")
    members = [math.prod(lax.axis_size(a) for a in axes) for axes in (local_axes, far_axes)]
    layer_out, totals = kernel_call(
        after_body,
        (
            jax.ShapeDtypeStruct((tok_rows, model_width), bf16),
            jax.ShapeDtypeStruct((members[0], 128), f32),
        ),
        "svvvvvvvvv",
        (2 * tok_rows * model_width * shortlist.shape[2], 4 << 20),
    )(facts, mid_states, own_part, *home, gain_rows, shortlist[0], student[0], targets[0][:, None])
    totals = lax.all_to_all(totals, local_axes, split_axis=0, concat_axis=0, tiled=True).sum(0)
    totals = jnp.broadcast_to(totals[None], (members[1], 128))
    totals = lax.all_to_all(totals, far_axes, split_axis=0, concat_axis=0, tiled=True).sum(0)
    return (layer_out[None], totals[0] / totals[1])


def solution(mesh):
    segments, expert_devices = mesh.devices.shape
    experts = 4
    fine = Mesh(
        mesh.devices.reshape(segments // 2, 2, experts, expert_devices // experts // ZL, ZL),
        ("y", "core", "x", "z4", "zl"),
    )
    seg, exp = ("y", "core"), ("x", "z4", "zl")
    placed = (
        P(seg, exp, None),
        P(seg, exp, None),
        P(seg, exp),
        P(seg, exp),
        P(seg, exp, None),
        P(seg, None, None),
        P(seg, None, None),
        P(seg, None, exp),
        P(seg, exp, None),
        P(seg, None, None),
        P(seg, exp, None),
        P(seg, exp),
    )
    return jax.shard_map(
        local,
        mesh=fine,
        in_specs=placed,
        out_specs=(P(seg, exp, None), P()),
        check_vma=False,
    )
```

```python
import functools
import math

import jax
import jax.numpy as jnp
from jax import lax
from jax.experimental import pallas as pl
from jax.experimental.pallas import tpu as pltpu
from jax.sharding import Mesh, PartitionSpec as P

HEADS = 16
HEAD_DIM = 128
LEN = 32
ZL = 4


epsilon = 1e-05
f32, bf16 = jnp.float32, jnp.bfloat16


def passed_along(block, axis, distance):
    devices = range(lax.axis_size(axis))
    route = [(i - distance, i) for i in devices if i - distance in devices]
    return lax.ppermute(block, axis, route)


def turned(block, axis, distance):
    count = math.prod(lax.axis_size(a) for a in ([axis] if isinstance(axis, str) else axis))
    return lax.ppermute(block, axis, [(i, (i + distance) % count) for i in range(count)])


def kernel_call(body, out_shape, in_specs, cost, limit=24 << 20):
    whole = pl.BlockSpec(memory_space=pltpu.VMEM)
    scalar = pl.BlockSpec(memory_space=pltpu.SMEM)
    return pl.pallas_call(
        body,
        out_shape=out_shape,
        in_specs=[scalar if k == "s" else whole for k in in_specs],
        out_specs=jax.tree.map(lambda _: whole, out_shape),
        cost_estimate=pl.CostEstimate(flops=cost[0], bytes_accessed=cost[1], transcendentals=0),
        compiler_params=pltpu.CompilerParams(vmem_limit_bytes=limit),
    )


def share_body(w_in, w_out, out, block_in, block_out, sems):
    width, hidden = w_in.shape
    half, deep = hidden // 2, width // 2
    first = pltpu.make_async_copy(w_in, block_in, sems.at[0])
    second = pltpu.make_async_copy(w_out, block_out, sems.at[1])
    first.start()
    second.start()
    first.wait()
    for h in range(2):
        for d in range(2):
            out[h, 0, :, d * half : (d + 1) * half] = block_in[
                d * deep : (d + 1) * deep, h * half : (h + 1) * half
            ]
    second.wait()
    for h in range(2):
        for p in range(width // hidden):
            out[h, 1, p * half : (p + 1) * half, :] = block_out[
                h * half : (h + 1) * half, p * hidden : (p + 1) * hidden
            ]


def relay_body(core, near, after, near_out, out, sem):
    del after, near_out
    copy = pltpu.make_async_copy(near.at[core[0]], out, sem)
    copy.start()
    copy.wait()


def mlp_body(rows, own, near_a, near_b, far_a, far_b, out, act):
    half = own.shape[3] // 2
    deep = own.shape[2]
    hidden = 2 * half
    pairs = (
        (own.at[0], own.at[1]),
        (near_a.at[0], near_a.at[1]),
        (near_b.at[0], near_b.at[1]),
        (far_a, far_b),
    )
    for k, (a, b) in enumerate(pairs):
        low = jnp.concatenate([a[0, :, :half], b[0, :, :half]], axis=1)
        high = jnp.concatenate([a[0, :, half:], b[0, :, half:]], axis=1)
        product = jnp.dot(rows[:, :deep], low, preferred_element_type=f32) + jnp.dot(
            rows[:, deep:], high, preferred_element_type=f32
        )
        act[:, k * hidden : (k + 1) * hidden] = jnp.maximum(product, 0.0).astype(bf16)
    for p in range(2 * deep // hidden):
        at = slice(p * half, (p + 1) * half)
        panel = jnp.concatenate([o[1, at, :] for pair in pairs for o in pair], axis=0)
        out[:, p * hidden : (p + 1) * hidden] = jnp.dot(
            act[...], panel, preferred_element_type=f32
        ).astype(bf16)


def normed_of(values, gain):
    centred = values - jnp.mean(values, axis=-1, keepdims=True)
    spread = jnp.mean(centred * centred, axis=-1, keepdims=True)
    return centred * lax.rsqrt(spread + epsilon) * gain


def before_body(facts, hidden, memory, gains, router, routes, mid, block):
    rows, width = hidden.shape
    states = hidden[...].astype(f32)
    queries = normed_of(states, gains[0:1, :]).astype(bf16)
    keys = memory[...]
    heads = [slice(h * HEAD_DIM, (h + 1) * HEAD_DIM) for h in range(HEADS)]
    scores = jnp.concatenate(
        [
            lax.dot_general(
                queries[:, h], keys[:, h], (((1,), (1,)), ((), ())), preferred_element_type=f32
            )
            for h in heads
        ],
        axis=0,
    ) * (1.0 / math.sqrt(HEAD_DIM))
    key_at = lax.broadcasted_iota(jnp.int32, scores.shape, 1)
    scores = jnp.where(key_at < facts[1], scores, -1e30)
    raised = jnp.exp(scores - jnp.max(scores, axis=-1, keepdims=True))
    weights = (raised / jnp.sum(raised, axis=-1, keepdims=True)).astype(bf16)
    attended = jnp.concatenate(
        [
            jnp.dot(weights[i * rows : (i + 1) * rows], keys[:, h], preferred_element_type=f32)
            for i, h in enumerate(heads)
        ],
        axis=1,
    )
    middle = states + jnp.where(facts[2] > 0, attended, 0.0)
    mid[...] = middle
    normed = normed_of(middle, gains[1:2, :]).astype(bf16)
    block[:, :width] = normed
    logits = lax.dot_general(
        normed, router[...], (((1,), (1,)), ((), ())), preferred_element_type=f32
    )
    lane = lax.broadcasted_iota(jnp.int32, logits.shape, 1)
    expert = lane % 8
    real = (expert < 4) & (lane < 16)
    logits = jnp.where(real, logits, -jnp.inf)
    raised = jnp.exp(logits - jnp.max(logits, axis=-1, keepdims=True))
    probs = raised / (0.5 * jnp.sum(raised, axis=-1, keepdims=True))
    first = jnp.where(real & (expert == routes[:, 0:1]), 1.0, 0.0)
    second = jnp.where(real & (expert == routes[:, 1:2]), 1.0, 0.0)
    prob_first = 0.5 * jnp.sum(probs * first, axis=-1, keepdims=True)
    prob_second = 0.5 * jnp.sum(probs * second, axis=-1, keepdims=True)
    gates = (prob_first * first + prob_second * second) / (prob_first + prob_second)
    token = lax.broadcasted_iota(jnp.int32, gates.shape, 0)
    gates = jnp.where(token < facts[0], gates, 0.0)
    upper = gates.astype(bf16).astype(f32)
    block[:, width:] = jnp.where(lane < 8, upper, gates - upper).astype(bf16)


def pack_body(slots, own, b1, b2, b3, rows, high, low):
    width = rows.shape[1]
    lanes = rows.shape[0]
    tokens = jnp.concatenate([own[...], b1[...], b2[...], b3[...]], axis=0)
    count = tokens.shape[0]
    aux = tokens[:, width:]
    lane = lax.broadcasted_iota(jnp.int32, (128, lanes), 1)
    part = lax.broadcasted_iota(jnp.int32, (128, lanes), 0)
    of_expert = lane // slots
    pick_high = (part == of_expert).astype(f32).astype(bf16)
    pick_low = (part == of_expert + 8).astype(f32).astype(bf16)
    gate_high = jnp.dot(aux, pick_high, preferred_element_type=f32)
    gate_low = jnp.dot(aux, pick_low, preferred_element_type=f32)
    chosen = gate_high > 0.0
    upto = (
        lax.broadcasted_iota(jnp.int32, (count, count), 0)
        >= lax.broadcasted_iota(jnp.int32, (count, count), 1)
    ).astype(f32).astype(bf16)
    rank = jnp.dot(upto, chosen.astype(f32).astype(bf16), preferred_element_type=f32)
    slot = (lax.broadcasted_iota(jnp.int32, (count, lanes), 1) % slots + 1).astype(f32)
    here = jnp.where(chosen & (rank == slot), 1.0, 0.0)
    rows[...] = lax.dot_general(
        here.astype(bf16), tokens[:, :width], (((0,), (0,)), ((), ())), preferred_element_type=f32
    ).astype(bf16)
    high[...] = (here * gate_high).astype(bf16)
    low[...] = (here * gate_low).astype(bf16)


def combine_body(rows, high, low, own, o1, o2, o3):
    value = jnp.dot(high[...], rows[...], preferred_element_type=f32) + jnp.dot(
        low[...], rows[...], preferred_element_type=f32
    )
    n = own.shape[0]
    own[...] = value[:n]
    for k, o in enumerate((o1, o2, o3)):
        o[...] = value[(k + 1) * n : (k + 2) * n].astype(bf16)


def after_body(
    facts, mid, own, p1, p2, p3, gains, shortlist, student, targets, out, totals
):
    def log_softmax(values):
        moved = values - jnp.max(values, axis=-1, keepdims=True)
        return moved - jnp.log(jnp.sum(jnp.exp(moved), axis=-1, keepdims=True))

    value = mid[...] + own[...]
    for p in (p1, p2, p3):
        value = value + p[...].astype(f32)
    layer = value.astype(bf16)
    out[...] = layer
    final = normed_of(layer.astype(f32), gains[2:3, :]).astype(bf16)
    teacher = log_softmax(jnp.dot(final, shortlist[...], preferred_element_type=f32))
    learner = log_softmax(student[...])
    column = lax.broadcasted_iota(jnp.int32, learner.shape, 1)
    picked = jnp.where(column == targets[...], learner, 0.0)
    token_loss = jnp.sum(jnp.exp(teacher) * (teacher - learner), axis=-1, keepdims=True) - jnp.sum(
        picked, axis=-1, keepdims=True
    )
    token = lax.broadcasted_iota(jnp.int32, token_loss.shape, 0)
    counted = (token < facts[0]) & (facts[2] > 0)
    loss_sum = jnp.sum(jnp.where(counted, token_loss, 0.0))
    loss_count = jnp.sum(jnp.where(counted, 1.0, 0.0))
    lane = lax.broadcasted_iota(jnp.int32, totals.shape, 1)
    totals[...] = jnp.where(lane == 0, loss_sum, jnp.where(lane == 1, loss_count, 0.0))


def local(
    hidden,
    memory,
    lengths,
    memory_lengths,
    routes,
    norm_gain,
    router,
    w_in,
    w_out,
    shortlist,
    student,
    targets,
):
    chips = lax.axis_size("y")
    experts = router.shape[2]
    tok_rows = hidden.shape[1]
    model_width = hidden.shape[2]
    capacity = 5 * tok_rows // 8
    decoder = lax.axis_index("y") >= chips // 2
    core = lax.axis_index("core").astype(jnp.int32)[None]
    model_hidden = w_in.shape[2]
    gain_rows = norm_gain[0]
    arrived, arrived_length = passed_along((memory[0], memory_lengths[0]), "y", chips // 2)
    router_rows = jnp.pad(router[0].T, ((0, 8 - experts), (0, 0)))
    router_rows = jnp.pad(jnp.concatenate([router_rows, router_rows], axis=0), ((0, 112), (0, 0)))
    whole = pl.BlockSpec(memory_space=pltpu.VMEM)
    scalars = pl.BlockSpec(memory_space=pltpu.SMEM)
    anywhere = pl.BlockSpec(memory_space=pl.ANY)
    piece = (2, model_width // 2, model_hidden)
    shared = pl.pallas_call(
        share_body,
        out_shape=jax.ShapeDtypeStruct((2,) + piece, bf16),
        in_specs=[anywhere] * 2,
        out_specs=whole,
        scratch_shapes=[
            pltpu.VMEM((model_width, model_hidden), bf16),
            pltpu.VMEM((model_hidden, model_width), bf16),
            pltpu.SemaphoreType.DMA((2,)),
        ],
        cost_estimate=pl.CostEstimate(flops=0, bytes_accessed=4 << 20, transcendentals=0),
        compiler_params=pltpu.CompilerParams(vmem_limit_bytes=56 << 20),
    )(w_in[0], w_out[0])
    line = lax.axis_size("z4") * lax.axis_size("zl")
    onward = [(i, (i - 1) % line) for i in range(line)] + [
        (line + i, line + (i + 1) % line) for i in range(line)
    ]
    facts = jnp.stack([lengths[0, 0], arrived_length[0], decoder.astype(jnp.int32)])
    mid_states, block = kernel_call(
        before_body,
        (
            jax.ShapeDtypeStruct((tok_rows, model_width), f32),
            jax.ShapeDtypeStruct((tok_rows, model_width + 128), bf16),
        ),
        "svvvvv",
        (4 * tok_rows * LEN * model_width, 1 << 20),
    )(facts, hidden[0], arrived, gain_rows, router_rows, routes[0])
    order = (2, 1, 3)
    visitors = [turned(block, "z4", k) for k in order]
    near_mine = lax.ppermute(shared, ("core", "z4", "zl"), onward)
    slots = 4 * capacity
    lanes = experts * slots
    packed, gates_high, gates_low = kernel_call(
        functools.partial(pack_body, slots),
        (
            jax.ShapeDtypeStruct((lanes, model_width), bf16),
            jax.ShapeDtypeStruct((4 * tok_rows, lanes), bf16),
            jax.ShapeDtypeStruct((4 * tok_rows, lanes), bf16),
        ),
        "vvvv",
        (2 * lanes * 4 * tok_rows * model_width, 2 << 20),
    )(block, *visitors)
    near_mine, relayed = pl.pallas_call(
        relay_body,
        out_shape=(
            jax.ShapeDtypeStruct((2,) + piece, bf16),
            jax.ShapeDtypeStruct(piece, bf16),
        ),
        in_specs=[scalars] + [anywhere] * 2,
        out_specs=(anywhere, whole),
        scratch_shapes=[pltpu.SemaphoreType.DMA],
        input_output_aliases={1: 0},
        cost_estimate=pl.CostEstimate(flops=0, bytes_accessed=2 << 20, transcendentals=0),
        compiler_params=pltpu.CompilerParams(vmem_limit_bytes=8 << 20),
    )(core, near_mine, gates_high)
    far_mine = lax.ppermute(relayed, ("core", "z4", "zl"), onward)
    crossing = [(i, (j + line) % (2 * line)) for i, j in onward]
    far_other = lax.ppermute(relayed, ("core", "z4", "zl"), crossing)
    near_other = turned(near_mine, "core", 1)
    rows = lax.all_to_all(packed, "x", split_axis=0, concat_axis=0, tiled=True)
    partial_out = pl.pallas_call(
        mlp_body,
        out_shape=jax.ShapeDtypeStruct((lanes, model_width), bf16),
        in_specs=[whole] * 6,
        out_specs=whole,
        scratch_shapes=[
            pltpu.VMEM((lanes, 4 * model_hidden), bf16),
        ],
        cost_estimate=pl.CostEstimate(
            flops=16 * lanes * model_width * model_hidden, bytes_accessed=11 << 20, transcendentals=0
        ),
        compiler_params=pltpu.CompilerParams(vmem_limit_bytes=24 << 20),
    )(rows, shared, near_mine, near_other, far_mine, far_other)
    returned = lax.all_to_all(partial_out, "x", split_axis=0, concat_axis=0, tiled=True)
    own_part, *parts = kernel_call(
        combine_body,
        (jax.ShapeDtypeStruct((tok_rows, model_width), f32),)
        + (jax.ShapeDtypeStruct((tok_rows, model_width), bf16),) * 3,
        "vvv",
        (4 * lanes * 4 * tok_rows * model_width, 2 << 20),
    )(returned, gates_high, gates_low)
    home = [turned(part, "z4", -k) for k, part in zip(order, parts)]
    local_axes, far_axes = ("core", "x", "zl"), ("y", "z4")
    members = [math.prod(lax.axis_size(a) for a in axes) for axes in (local_axes, far_axes)]
    layer_out, totals = kernel_call(
        after_body,
        (
            jax.ShapeDtypeStruct((tok_rows, model_width), bf16),
            jax.ShapeDtypeStruct((members[0], 128), f32),
        ),
        "svvvvvvvvv",
        (2 * tok_rows * model_width * shortlist.shape[2], 4 << 20),
    )(facts, mid_states, own_part, *home, gain_rows, shortlist[0], student[0], targets[0][:, None])
    totals = lax.all_to_all(totals, local_axes, split_axis=0, concat_axis=0, tiled=True).sum(0)
    totals = jnp.broadcast_to(totals[None], (members[1], 128))
    totals = lax.all_to_all(totals, far_axes, split_axis=0, concat_axis=0, tiled=True).sum(0)
    return (layer_out[None], totals[0] / totals[1])


def solution(mesh):
    segments, expert_devices = mesh.devices.shape
    experts = 4
    fine = Mesh(
        mesh.devices.reshape(segments // 2, 2, experts, expert_devices // experts // ZL, ZL),
        ("y", "core", "x", "z4", "zl"),
    )
    seg, exp = ("y", "core"), ("x", "z4", "zl")
    placed = (
        P(seg, exp, None),
        P(seg, exp, None),
        P(seg, exp),
        P(seg, exp),
        P(seg, exp, None),
        P(seg, None, None),
        P(seg, None, None),
        P(seg, None, exp),
        P(seg, exp, None),
        P(seg, None, None),
        P(seg, exp, None),
        P(seg, exp),
    )
    return jax.shard_map(
        local,
        mesh=fine,
        in_specs=placed,
        out_specs=(P(seg, exp, None), P()),
        check_vma=False,
    )
```
